128 devices in a mesh: fsdp: 16 (over y, z), tp: 8 (over x, core).
Axes of the slice: x: 4, y: 4, z: 4, core: 2. Of those that a mesh axis runs over, the one named last changes fastest.
Arguments:
- gradient: bfloat16 [8192, 14336], P('fsdp', 'tp'), may hold values from -6 to 6
- momentum: float32 [8192, 14336], P('fsdp', 'tp')
- basis: float32 [14336, 1024], P(('tp', 'fsdp')), may hold values from -0.046875 to 0.046875
Outputs:
- new_momentum: float32 [8192, 14336], P('fsdp', 'tp')
- new_basis: float32 [14336, 1024], P(('tp', 'fsdp'))
- update: bfloat16 [8192, 14336], P('fsdp', 'tp')
The draws below stay inside these ranges and needn't reach their ends.
All inputs are finite; a program needn't handle non-finite values.
Results may differ from the reference program's by a relative error of at most 0.0023.
Values sent between devices are 32-bit elements; how exact they have to be, the bound alone decides.
A program may use at most 128 MiB of HBM per device.

```python
import jax
import jax.numpy as jnp
from jax import lax

M = 8192
N = 14336
RANK = 1024


def draw_momentum(key, part):
    key = jax.random.fold_in(key, 7)
    kbase, krow, kcol = jax.random.split(key, 3)
    base = jax.random.normal(kbase, (M, N), jnp.float32)
    colscale = jnp.exp(jax.random.uniform(kcol, (1, N), jnp.float32, 0.0, 2.3))
    rise = jnp.exp(1.1 * jnp.arange(M, dtype=jnp.float32) / M)[:, None]
    rowscale = jnp.exp(jax.random.uniform(krow, (M, 1), jnp.float32, 0.0, 1.2))
    return 0.5 * base * rise * rowscale * colscale


def level_of(stream_key, dims, shards, least, top_value):
    def one(axis_at, parts):
        steps = jax.random.uniform(jax.random.fold_in(jax.random.fold_in(stream_key, 6), axis_at), (parts,), jnp.float32, least / len(shards), top_value / len(shards))
        return jnp.repeat(jnp.exp(steps), dims[axis_at] // parts).reshape((-1,) + (1,) * (len(dims) - axis_at - 1))

    level = one(*shards[0])
    for cut in shards[1:]:
        level = level * one(*cut)
    return level


def gaussian(own_key, dims, spread, limit, pieces=(), kind=jnp.bfloat16):
    drawn = jax.random.normal(own_key, dims, jnp.float32) * spread
    if len(pieces) > 0:
        drawn = level_of(own_key, dims, pieces, -0.22, 0.18) * drawn
    return jnp.clip(drawn, min=-limit, max=limit).astype(kind)


def setup_inputs(seed: int = 0) -> dict:
    splits = jax.random.split(jax.random.key(seed), 4)
    return {
        "gradient": gaussian(splits[0], (M, N), 1.0, 6.0, ((0, 16), (1, 8))),
        "momentum": draw_momentum(jax.random.fold_in(splits[3], 71), 0),
        "basis": gaussian(splits[2], (N, RANK), N ** -0.5, 0.046875, ((0, 128),), jnp.float32),
    }


def mmul(a, b):
    return jnp.dot(a.astype(jnp.float32), b.astype(jnp.float32), precision=lax.Precision.HIGHEST, preferred_element_type=jnp.float32)

def reference(gradient, momentum, basis):
    mixed = momentum + gradient.astype(jnp.float32)
    left = mmul(mixed, basis)
    gram = mmul(left.T, left)
    lower = jnp.linalg.cholesky(gram)
    ortho = lax.linalg.triangular_solve(lower, left, left_side=False, lower=True, transpose_a=True)
    right = mmul(mixed.T, ortho)
    colnorm = jnp.sqrt(lax.optimization_barrier(jnp.sum(right * right, axis=0)) + 1e-08)
    new_basis = right / colnorm
    new_momentum = mixed - 0.05 * mmul(ortho, right.T)
    factor = jnp.sqrt(jnp.float32(M) * jnp.float32(N) / jnp.float32(RANK))
    update = (factor * mmul(ortho, new_basis.T)).astype(jnp.bfloat16)
    return (new_momentum, new_basis, update)
```

```python
import functools

import jax
import jax.numpy as jnp
from jax import lax
from jax.experimental import pallas as pl
from jax.experimental.pallas import tpu as pltpu
from jax.sharding import PartitionSpec as P

M = 8192
N = 14336
RANK = 1024
BLOCK = 128
STRIP = 8
HIGHEST = lax.Precision.HIGHEST
HIGH = lax.Precision.HIGH


def dot(a, b, ca, cb, precision):
    dims = (((ca,), (cb,)), ((), ()))
    return lax.dot_general(a, b, dims, precision=precision, preferred_element_type=jnp.float32)


def recip(d):
    r = pl.reciprocal(d, approx=True)
    r = r * (2.0 - d * r)
    return r * (2.0 - d * r)


def factor(block):
    shape = (STRIP, BLOCK)
    lane = lax.broadcasted_iota(jnp.int32, shape, 1)
    sub = lax.broadcasted_iota(jnp.int32, shape, 0)
    count = BLOCK // STRIP
    strips = [block[STRIP * t : STRIP * (t + 1), :] for t in range(count)]
    out = []
    for s in range(count):
        first = STRIP * s
        w = strips[s]
        columns = [jnp.broadcast_to(w[:, first + j : first + j + 1], shape) for j in range(STRIP)]
        a = [[jnp.broadcast_to(columns[j][i : i + 1, :], shape) for j in range(i + 1)] for i in range(STRIP)]
        pivots = jnp.ones(shape, jnp.float32)
        for k in range(STRIP):
            here = lane == first + k
            inverse = recip(a[k][k])
            pivots = jnp.where(sub == k, a[k][k], pivots)
            ratio = {i: a[i][k] * inverse for i in range(k + 1, STRIP)}
            for i in range(k + 1, STRIP):
                for j in range(k + 1, i + 1):
                    a[i][j] = a[i][j] - ratio[i] * a[j][k]
            times = jnp.zeros(shape, jnp.float32)
            for i in range(k + 1, STRIP):
                times = jnp.where(sub == i, ratio[i], times)
            w = jnp.where(here & (sub >= k), jnp.where(sub == k, 1.0, 0.0), w)
            w = w - times * jnp.broadcast_to(w[k : k + 1, :], shape)
        r = w * lax.rsqrt(pivots)
        r = jnp.where((lane > first + sub) & (lane < first + STRIP), 0.0, r)
        out.append(jnp.where(lane <= sub + first, r, 0.0))
        inside = (lane >= first) & (lane < first + STRIP)
        turned = jnp.transpose(r)
        rows = [jnp.broadcast_to(r[i : i + 1, :], shape) for i in range(STRIP)]
        for t in range(s + 1, count):
            total = jnp.where(inside, 0.0, strips[t])
            for i in range(STRIP):
                total = total - jnp.broadcast_to(turned[STRIP * t : STRIP * (t + 1), i : i + 1], shape) * rows[i]
            strips[t] = total
    return jnp.concatenate(out, axis=0)


def inverse_kernel(gram_ref, out_ref, held):
    n = held.shape[0]
    held[...] = gram_ref[...]
    shape = (BLOCK, BLOCK)
    eye = (lax.broadcasted_iota(jnp.int32, shape, 0) == lax.broadcasted_iota(jnp.int32, shape, 1)).astype(jnp.float32)
    lanes = lax.broadcasted_iota(jnp.int32, (BLOCK, n), 1)

    def step(k, carry):
        mine = pl.ds(pl.multiple_of(k * BLOCK, BLOCK), BLOCK)
        inverse = factor(held[mine, mine])
        held[mine, mine] = eye
        held[mine, :] = dot(inverse, held[mine, :], 1, 0, HIGHEST)
        out_ref[mine, :] = jnp.where(lanes < (k + 1) * BLOCK, held[mine, :], 0.0)

        def below(t, inner):
            rows = pl.ds(pl.multiple_of(t * BLOCK, BLOCK), BLOCK)
            held[rows, mine] = jnp.zeros(shape, jnp.float32)
            held[rows, :] = held[rows, :] - dot(held[mine, rows], held[mine, :], 0, 0, HIGHEST)
            return inner

        lax.fori_loop(k + 1, n // BLOCK, below, 0)
        return carry

    lax.fori_loop(0, n // BLOCK, step, 0)


def cholesky_inverse(gram):
    return pl.pallas_call(
        inverse_kernel,
        out_shape=jax.ShapeDtypeStruct(gram.shape, jnp.float32),
        in_specs=[pl.BlockSpec(memory_space=pltpu.VMEM)],
        out_specs=pl.BlockSpec(memory_space=pltpu.VMEM),
        scratch_shapes=[pltpu.VMEM(gram.shape, jnp.float32)],
        compiler_params=pltpu.CompilerParams(vmem_limit_bytes=32 << 20),
        cost_estimate=pl.CostEstimate(flops=60_000_000_000, bytes_accessed=8 << 20, transcendentals=0),
        name="cholesky_inverse",
    )(gram)


def local(gradient, momentum, basis):
    mixed = momentum + gradient.astype(jnp.float32)
    left = lax.psum(dot(mixed, lax.all_gather(basis, "fsdp", axis=0, tiled=True), 1, 0, HIGH), "tp")
    part = lax.axis_index("tp") * BLOCK
    gram_part = dot(left, lax.dynamic_slice_in_dim(left, part, BLOCK, 1), 0, 0, HIGHEST)
    gram = lax.all_gather(lax.psum(gram_part.T, "fsdp"), "tp", axis=0, tiled=True)
    cross_mine = lax.psum_scatter(dot(mixed, left, 0, 0, HIGH), "fsdp", scatter_dimension=0, tiled=True)
    cross = lax.all_gather(cross_mine, "fsdp", axis=0, tiled=True)
    inverse = cholesky_inverse(gram)
    right = dot(cross, inverse, 1, 1, HIGH)
    ortho = dot(left, inverse, 1, 1, HIGH)
    squares = lax.psum(jnp.sum(right * right, axis=0), "tp")
    new_momentum = mixed - 0.05 * dot(ortho, right, 1, 1, lax.Precision.DEFAULT)
    colnorm = jnp.sqrt(squares + 1e-08)
    new_basis = dot(cross_mine, inverse, 1, 1, HIGH) / colnorm
    factor = jnp.sqrt(jnp.float32(M) * jnp.float32(N) / jnp.float32(RANK))
    update = dot(factor * ortho / colnorm, right, 1, 1, HIGH).astype(jnp.bfloat16)
    return (new_momentum, new_basis, update)


def solution(mesh):
    placed = (P("fsdp", "tp"), P("fsdp", "tp"), P(("tp", "fsdp"), None))
    return jax.shard_map(
        local,
        mesh=mesh,
        in_specs=placed,
        out_specs=(P("fsdp", "tp"), P(("tp", "fsdp"), None), P("fsdp", "tp")),
        check_vma=False,
    )
```

```python
import functools

import jax
import jax.numpy as jnp
from jax import lax
from jax.experimental import pallas as pl
from jax.experimental.pallas import tpu as pltpu
from jax.sharding import PartitionSpec as P

M = 8192
N = 14336
RANK = 1024
BLOCK = 128
STRIP = 8
HIGHEST = lax.Precision.HIGHEST
HIGH = lax.Precision.HIGH
MESH = pl.DeviceIdType.MESH
SHARD = 112
HALF = 56
WIDE = 512


def dot(a, b, ca, cb, precision):
    dims = (((ca,), (cb,)), ((), ()))
    return lax.dot_general(a, b, dims, precision=precision, preferred_element_type=jnp.float32)


def recip(d):
    r = pl.reciprocal(d, approx=True)
    r = r * (2.0 - d * r)
    return r * (2.0 - d * r)


def factor(block, pause):
    shape = (STRIP, BLOCK)
    lane = lax.broadcasted_iota(jnp.int32, shape, 1)
    sub = lax.broadcasted_iota(jnp.int32, shape, 0)
    count = BLOCK // STRIP
    strips = [block[STRIP * t : STRIP * (t + 1), :] for t in range(count)]
    out = []
    for s in range(count):
        if s in (4, 8, 12):
            pause()
        first = STRIP * s
        w = strips[s]
        columns = [jnp.broadcast_to(w[:, first + j : first + j + 1], shape) for j in range(STRIP)]
        a = [[jnp.broadcast_to(columns[j][i : i + 1, :], shape) for j in range(i + 1)] for i in range(STRIP)]
        pivots = jnp.ones(shape, jnp.float32)
        for k in range(STRIP):
            here = lane == first + k
            inverse = recip(a[k][k])
            pivots = jnp.where(sub == k, a[k][k], pivots)
            ratio = {i: a[i][k] * inverse for i in range(k + 1, STRIP)}
            for i in range(k + 1, STRIP):
                for j in range(k + 1, i + 1):
                    a[i][j] = a[i][j] - ratio[i] * a[j][k]
            times = jnp.zeros(shape, jnp.float32)
            for i in range(k + 1, STRIP):
                times = jnp.where(sub == i, ratio[i], times)
            w = jnp.where(here & (sub >= k), jnp.where(sub == k, 1.0, 0.0), w)
            w = w - times * jnp.broadcast_to(w[k : k + 1, :], shape)
        r = w * lax.rsqrt(pivots)
        r = jnp.where((lane > first + sub) & (lane < first + STRIP), 0.0, r)
        out.append(jnp.where(lane <= sub + first, r, 0.0))
        inside = (lane >= first) & (lane < first + STRIP)
        turned = jnp.transpose(r)
        rows = [jnp.broadcast_to(r[i : i + 1, :], shape) for i in range(STRIP)]
        for t in range(s + 1, count):
            total = jnp.where(inside, 0.0, strips[t])
            for i in range(STRIP):
                total = total - jnp.broadcast_to(turned[STRIP * t : STRIP * (t + 1), i : i + 1], shape) * rows[i]
            strips[t] = total
    return jnp.concatenate(out, axis=0)


def split(x):
    high = x.astype(jnp.bfloat16)
    return high, (x - high.astype(jnp.float32)).astype(jnp.bfloat16)


def dot3(ah, al, bh, bl, ca, cb):
    def one(a, b):
        dims = (((ca,), (cb,)), ((), ()))
        return lax.dot_general(a, b, dims, preferred_element_type=jnp.float32)

    return one(ah, bh) + (one(ah, bl) + one(al, bh))


class Net:
    def __init__(self, send_sem, recv_sem):
        self.send_sem, self.recv_sem, self.made, self.open = send_sem, recv_sem, {}, []
        self.index, self.dry = {}, False
        fsdp, tp = lax.axis_index("fsdp"), lax.axis_index("tp")
        self.y, self.z = fsdp // 4, fsdp % 4
        self.x, self.core = tp // 2, tp % 2

    def at(self, y=0, z=0, x=0, core=0):
        f = ((self.y + y + 4) % 4) * 4 + (self.z + z + 4) % 4
        t = ((self.x + x + 4) % 4) * 2 + (self.core + core) % 2
        return (f, t)

    def send(self, key, source, target, to):
        i = self.index.setdefault(key, len(self.index))

        def make():
            return pltpu.make_async_remote_copy(
                src_ref=source(),
                dst_ref=target(),
                send_sem=self.send_sem.at[i],
                recv_sem=self.recv_sem.at[i],
                device_id=self.at(**to),
                device_id_type=MESH,
            )

        self.made[key] = make
        if not self.dry:
            self.open.append(key)
            make().start()

    def got(self, *keys):
        for key in () if self.dry else keys:
            self.made[key]().wait_recv()

    def sent(self, name=None):
        done = [key for key in self.open if name is None or key[0] == name]
        for key in done:
            self.made[key]().wait_send()
        self.open = [key for key in self.open if key not in done]


def shard_of(net, ref, first, o1, o2, half, part):
    dy, dz = (o1, o2) if first == "y" else (o2, o1)
    index = ((net.y + dy + 4) % 4) * 4 + (net.z + dz + 4) % 4
    at, rows = {"all": (0, SHARD), "top": (0, HALF), "low": (HALF, HALF)}[part]
    return ref.at[pl.ds(pl.multiple_of(index * SHARD + at, 8), rows), pl.ds(half * WIDE, WIDE)]


def gather_events(net, name, own, buf):
    lists = []
    for half, (d1, d2) in enumerate((("y", "z"), ("z", "y"))):
        key = lambda *k, half=half: (name, half) + k
        shard = lambda o1, o2, part="all", d1=d1, half=half: shard_of(net, buf, d1, o1, o2, half, part)

        def both(o, key=key, shard=shard, d2=d2):
            for way, sign in ((1, "+"), (-1, "-")):
                net.send(key(2, o, sign), lambda: shard(o, 0), lambda: shard(o, 0), {d2: way})

        def start(key=key, shard=shard, d1=d1, d2=d2, half=half):
            mine = lambda: own(half)
            for way, sign in ((1, "+"), (-1, "-")):
                net.send(key(1, sign), mine, lambda: shard(0, 0), {d1: way})
            for way, sign in ((1, "+"), (-1, "-")):
                net.send(key(2, 0, sign), mine, lambda: shard(0, 0), {d2: way})

        def near(o, way, sign, part, key=key, shard=shard, d1=d1, both=both):
            net.got(key(1, sign))
            net.send(key(1, "f" + sign), lambda: shard(o, 0, part), lambda: shard(o, 0, part), {d1: way})
            both(o)

        def far(key=key, both=both):
            net.got(key(1, "f+"), key(1, "f-"))
            both(2)

        def pass_on(o, p, way, sign, part, key=key, shard=shard, d2=d2):
            net.got(key(2, o, sign))
            net.send(key(2, o, "f" + sign), lambda: shard(o, p, part), lambda: shard(o, p, part), {d2: way})

        def last(key=key):
            for o in (0, -1, 1, 2):
                net.got(key(2, o, "f+"), key(2, o, "f-"))

        events = [start, functools.partial(near, -1, 1, "+", "top"), functools.partial(near, 1, -1, "-", "low")]
        for i, o in enumerate((0, -1, 1, 2)):
            if i == 1:
                events.append(far)
            events.append(functools.partial(pass_on, o, -1, 1, "+", "top"))
            events.append(functools.partial(pass_on, o, 1, -1, "-", "low"))
        events.append(last)
        lists.append(events)
    return [e for pair in zip(*lists) for e in pair]


def scatter_events(net, name, buf, ra, rb, rc, rd):
    lists = []
    order = (2, 1, -1, 0)
    for half, (e1, e2) in enumerate((("y", "z"), ("z", "y"))):
        key = lambda *k, half=half: (name, half) + k
        shard = lambda o1, o2, part="all", e1=e1, half=half: shard_of(net, buf, e1, o1, o2, half, part)

        def add(ref, *others):
            if net.dry:
                return
            total = ref[...]
            for other in others:
                total = total + other[...]
            ref[...] = total

        def start(o, key=key, shard=shard, e1=e1, half=half):
            i = (half * 4 + order.index(o)) * 2
            net.send(key(1, o, "f+"), lambda: shard(2, o, "top"), lambda: ra.at[i], {e1: 1})
            net.send(key(1, o, "f-"), lambda: shard(2, o, "low"), lambda: ra.at[i + 1], {e1: -1})

        def near(o, way, sign, part, j, key=key, shard=shard, e1=e1, half=half):
            i = (half * 4 + order.index(o)) * 2 + j
            net.got(key(1, o, "f" + sign))
            add(shard(way, o, part), ra.at[i])
            net.send(key(1, o, sign), lambda: shard(way, o), lambda: rb.at[i], {e1: way})

        def line(o, key=key, shard=shard, half=half):
            i = (half * 4 + order.index(o)) * 2
            net.got(key(1, o, "+"), key(1, o, "-"))
            add(shard(0, o), rb.at[i], rb.at[i + 1])

        def far(key=key, shard=shard, e2=e2, half=half, line=line):
            line(2)
            net.send(key(2, "f+"), lambda: shard(0, 2, "top"), lambda: rc.at[2 * half], {e2: 1})
            net.send(key(2, "f-"), lambda: shard(0, 2, "low"), lambda: rc.at[2 * half + 1], {e2: -1})

        def side(way, sign, part, j, key=key, shard=shard, e2=e2, half=half, line=line):
            line(way)
            net.got(key(2, "f" + sign))
            add(shard(0, way, part), rc.at[2 * half + j])
            net.send(key(2, sign), lambda: shard(0, way), lambda: rd.at[2 * half + j], {e2: way})

        def mine(key=key, shard=shard, half=half, line=line):
            line(0)
            net.got(key(2, "+"), key(2, "-"))
            add(shard(0, 0), rd.at[2 * half], rd.at[2 * half + 1])

        events = [functools.partial(start, o) for o in order]
        for o in order:
            events.append(functools.partial(near, o, 1, "+", "top", 0))
            events.append(functools.partial(near, o, -1, "-", "low", 1))
            if o == 1:
                events.append(far)
        events.append(functools.partial(side, 1, "+", "top", 0))
        events.append(functools.partial(side, -1, "-", "low", 1))
        events.append(mine)
        lists.append(events)
    return [e for pair in zip(*lists) for e in pair]


def tp_gather_events(net, name, ref, piece, start_of):
    def part(dx, which="all"):
        at, rows = {"all": (0, piece), "top": (0, piece // 2), "low": (piece // 2, piece // 2)}[which]
        return ref.at[pl.ds(pl.multiple_of(start_of(dx) + at, 8), rows), :]

    def put(key, dx, which, to):
        net.send((name,) + key, lambda: part(dx, which), lambda: part(dx, which), to)

    def start():
        put(("+",), 0, "all", {"x": 1})
        put(("-",), 0, "all", {"x": -1})
        put(("c", 0), 0, "all", {"core": 1})

    def near():
        net.got((name, "+"))
        put(("f+",), -1, "top", {"x": 1})
        net.got((name, "-"))
        put(("f-",), 1, "low", {"x": -1})
        put(("c", -1), -1, "all", {"core": 1})
        put(("c", 1), 1, "all", {"core": 1})

    def last():
        net.got((name, "f+"), (name, "f-"))
        put(("c", 2), 2, "all", {"core": 1})
        net.got(*[(name, "c", dx) for dx in (0, -1, 1, 2)])

    return start, near, last


def tp_sum(net, ref, out, lc, la, lb):
    mine = net.core * 256
    other = 256 - mine
    net.send(("core",), lambda: ref.at[pl.ds(pl.multiple_of(other, 8), 256), :], lambda: lc, {"core": 1})
    net.got(("core",))
    rows = pl.ds(pl.multiple_of(mine, 8), 256)
    ref[rows, :] = ref[rows, :] + lc[...]

    def start_of(dx):
        return mine + ((net.x + dx + 4) % 4) * 64

    def piece(dx, at=0, count=64):
        return ref.at[pl.ds(pl.multiple_of(start_of(dx) + at, 8), count), :]

    net.send(("xf+",), lambda: piece(2, 0, 32), lambda: la.at[0], {"x": 1})
    net.send(("xf-",), lambda: piece(2, 32, 32), lambda: la.at[1], {"x": -1})
    for way, sign, at, j in ((1, "+", 0, 0), (-1, "-", 32, 1)):
        net.got(("xf" + sign,))
        there = piece(way, at, 32)
        there[...] = there[...] + la[j]
        net.send(("x" + sign,), lambda way=way: piece(way), lambda j=j: lb.at[j], {"x": way})
    net.got(("x+",), ("x-",))
    out[pl.ds(pl.multiple_of(start_of(0), 8), 64), :] = piece(0)[...] + lb[0] + lb[1]
    for event in tp_gather_events(net, "left", out, 64, start_of):
        event()


def main_kernel(
    momentum_ref, gradient_ref, basis_ref, left_ref, cross_ref, inverse_ref,
    buf, mh, ml, lbuf, lc, la, lb, lh, ll, ra, rb, rc, rd, held, gpart, gsum, send_sem, recv_sem,
):
    net = Net(send_sem, recv_sem)
    me = net.y * 4 + net.z
    tp = net.x * 2 + net.core
    barrier = pltpu.get_barrier_semaphore()
    for i in range(1, 16):
        pl.semaphore_signal(barrier, inc=1, device_id=((me + i) % 16, tp), device_id_type=MESH)
    near = ({"x": 1}, {"x": -1}, {"core": 1})
    for to in near:
        pl.semaphore_signal(barrier, inc=1, device_id=net.at(**to), device_id_type=MESH)
    pl.semaphore_wait(barrier, 15 + len(near))

    events = gather_events(net, "basis", lambda half: basis_ref.at[:, pl.ds(half * WIDE, WIDE)], buf)
    for event in events[:2]:
        event()
    buf[pl.ds(pl.multiple_of(me * SHARD, 8), SHARD), :] = basis_ref[...]

    @pl.loop(0, 16)
    def _(i):
        rows = pl.ds(pl.multiple_of(i * 32, 32), 32)
        mh[rows, :], ml[rows, :] = split(momentum_ref[rows, :] + gradient_ref[rows, :].astype(jnp.float32))

    for event in events[2:]:
        event()

    @pl.loop(0, 4)
    def _(i):
        columns = pl.ds(pl.multiple_of(i * 256, 256), 256)
        bh, bl = split(buf[:, columns])
        lbuf[:, columns] = dot3(mh[...], ml[...], bh, bl, 1, 0)

    tp_sum(net, lbuf, left_ref, lc, la, lb)
    net.sent()

    own_rows = pl.ds(pl.multiple_of(tp * BLOCK, BLOCK), BLOCK)
    gpart[...] = dot(left_ref[:, own_rows], left_ref[...], 0, 0, HIGHEST)
    copies = []
    for i in range(1, 16):
        to = (me + i) % 16
        copies.append(
            pltpu.make_async_remote_copy(
                src_ref=gpart.at[pl.ds(pl.multiple_of(to * 8, 8), 8), :],
                dst_ref=gsum.at[i],
                send_sem=send_sem.at[150 + i],
                recv_sem=recv_sem.at[150 + i],
                device_id=(to, tp),
                device_id_type=MESH,
            )
        )
        copies[-1].start()

    lh[...], ll[...] = split(left_ref[...])

    @pl.loop(0, 7)
    def _(i):
        columns = pl.ds(pl.multiple_of(i * 256, 256), 256)
        buf[columns, :] = dot3(mh[:, columns], ml[:, columns], lh[...], ll[...], 0, 0)

    scatter = scatter_events(net, "scatter", buf, ra, rb, rc, rd)
    for event in scatter[:8]:
        event()
    for copy in copies:
        copy.wait()
    total = gpart[pl.ds(pl.multiple_of(me * 8, 8), 8), :]
    for i in range(1, 16):
        total = total + gsum[i]
    at = pl.multiple_of(tp * BLOCK + me * 8, 8)
    held[pl.ds(at, 8), :] = total
    copies = []
    for i in range(1, 16):
        copies.append(
            pltpu.make_async_remote_copy(
                src_ref=held.at[pl.ds(at, 8), :],
                dst_ref=held.at[pl.ds(at, 8), :],
                send_sem=send_sem.at[170 + i],
                recv_sem=recv_sem.at[170 + i],
                device_id=((me + i) % 16, tp),
                device_id_type=MESH,
            )
        )
        copies[-1].start()
    for event in scatter[8:12]:
        event()
    for copy in copies:
        copy.wait()
    gram_events = tp_gather_events(
        net, "gram", held, BLOCK, lambda dx: (((net.x + dx + 4) % 4) * 2 + net.core) * BLOCK
    )
    gram_events[0]()
    for event in scatter[12:18]:
        event()
    gram_events[1]()
    for event in scatter[18:22]:
        event()
    gram_events[2]()
    net.sent("gram")

    def own(half):
        return shard_of(net, buf, "y", 0, 0, half, "all")

    def keep():
        if net.dry:
            return
        rows = pl.ds(pl.multiple_of(me * SHARD, 8), SHARD)
        cross_ref[rows, :] = buf[rows, :]

    rest = scatter[22:] + [keep] + gather_events(net, "cross", own, cross_ref)
    eliminate(net, held, inverse_ref, rest)
    net.sent()


def eliminate(net, held, out_ref, events):
    n = held.shape[0]
    count = n // BLOCK
    shape = (BLOCK, BLOCK)
    eye = (lax.broadcasted_iota(jnp.int32, shape, 0) == lax.broadcasted_iota(jnp.int32, shape, 1)).astype(jnp.float32)
    lanes = lax.broadcasted_iota(jnp.int32, (BLOCK, n), 1)
    slots = 5 * count
    plan = [events[len(events) * i // slots : len(events) * (i + 1) // slots] for i in range(slots)]
    net.dry = True
    for event in events:
        event()
    net.dry = False

    def step(k, carry):
        used = []

        def pause():
            for i in range(count):
                group = plan[5 * i + len(used)]
                if group:

                    @pl.when(k == i)
                    def _():
                        for event in group:
                            event()

            used.append(None)

        mine = pl.ds(pl.multiple_of(k * BLOCK, BLOCK), BLOCK)
        pause()
        inverse = factor(held[mine, mine], pause)
        held[mine, mine] = eye
        held[mine, :] = dot(inverse, held[mine, :], 1, 0, HIGHEST)
        out_ref[mine, :] = jnp.where(lanes < (k + 1) * BLOCK, held[mine, :], 0.0)
        pause()

        def below(t, inner):
            rows = pl.ds(pl.multiple_of(t * BLOCK, BLOCK), BLOCK)
            held[rows, mine] = jnp.zeros(shape, jnp.float32)
            held[rows, :] = held[rows, :] - dot(held[mine, rows], held[mine, :], 0, 0, HIGHEST)
            return inner

        lax.fori_loop(k + 1, count, below, 0)
        return carry

    lax.fori_loop(0, count, step, 0)


def factors(momentum, gradient, basis):
    f32, bf16 = jnp.float32, jnp.bfloat16
    rows, columns = momentum.shape
    vmem = pl.BlockSpec(memory_space=pltpu.VMEM)
    return pl.pallas_call(
        main_kernel,
        out_shape=[
            jax.ShapeDtypeStruct((rows, RANK), f32),
            jax.ShapeDtypeStruct((columns, RANK), f32),
            jax.ShapeDtypeStruct((RANK, RANK), f32),
        ],
        in_specs=[vmem] * 3,
        out_specs=[vmem] * 3,
        scratch_shapes=[
            pltpu.VMEM((columns, RANK), f32),
            pltpu.VMEM((rows, columns), bf16),
            pltpu.VMEM((rows, columns), bf16),
            pltpu.VMEM((rows, RANK), f32),
            pltpu.VMEM((256, RANK), f32),
            pltpu.VMEM((2, 32, RANK), f32),
            pltpu.VMEM((2, 64, RANK), f32),
            pltpu.VMEM((rows, RANK), bf16),
            pltpu.VMEM((rows, RANK), bf16),
            pltpu.VMEM((16, HALF, WIDE), f32),
            pltpu.VMEM((16, SHARD, WIDE), f32),
            pltpu.VMEM((4, HALF, WIDE), f32),
            pltpu.VMEM((4, SHARD, WIDE), f32),
            pltpu.VMEM((RANK, RANK), f32),
            pltpu.VMEM((BLOCK, RANK), f32),
            pltpu.VMEM((16, 8, RANK), f32),
            pltpu.SemaphoreType.DMA((192,)),
            pltpu.SemaphoreType.DMA((192,)),
        ],
        compiler_params=pltpu.CompilerParams(
            collective_id=0, has_side_effects=True, vmem_limit_bytes=62 << 20
        ),
        cost_estimate=pl.CostEstimate(flops=60_000_000_000, bytes_accessed=30 << 20, transcendentals=0),
        name="factors",
    )(momentum, gradient, basis)


def local(gradient, momentum, basis):
    mixed = momentum + gradient.astype(jnp.float32)
    left, cross, inverse = factors(momentum, gradient, basis)
    right = dot(cross, inverse, 1, 1, HIGH)
    ortho = dot(left, inverse, 1, 1, HIGH)
    squares = lax.psum(jnp.sum(right * right, axis=0), "tp")
    new_momentum = mixed - 0.05 * dot(ortho, right, 1, 1, lax.Precision.DEFAULT)
    colnorm = jnp.sqrt(squares + 1e-08)
    first = lax.axis_index("fsdp") * SHARD
    new_basis = lax.dynamic_slice_in_dim(right, first, SHARD, 0) / colnorm
    scale = jnp.sqrt(jnp.float32(M) * jnp.float32(N) / jnp.float32(RANK))
    update = dot(scale * ortho / colnorm, right, 1, 1, HIGH).astype(jnp.bfloat16)
    return (new_momentum, new_basis, update)


def solution(mesh):
    placed = (P("fsdp", "tp"), P("fsdp", "tp"), P(("tp", "fsdp"), None))
    return jax.shard_map(
        local,
        mesh=mesh,
        in_specs=placed,
        out_specs=(P("fsdp", "tp"), P(("tp", "fsdp"), None), P("fsdp", "tp")),
        check_vma=False,
    )
```

```python
import functools

import jax
import jax.numpy as jnp
from jax import lax
from jax.experimental import pallas as pl
from jax.experimental.pallas import tpu as pltpu
from jax.sharding import PartitionSpec as P

M = 8192
N = 14336
RANK = 1024
BLOCK = 128
STRIP = 8
HIGHEST = lax.Precision.HIGHEST
HIGH = lax.Precision.HIGH
MESH = pl.DeviceIdType.MESH
SHARD = 112
HALF = 56
WIDE = 512


def dot(a, b, ca, cb, precision):
    dims = (((ca,), (cb,)), ((), ()))
    return lax.dot_general(a, b, dims, precision=precision, preferred_element_type=jnp.float32)


def recip(d):
    r = pl.reciprocal(d, approx=True)
    r = r * (2.0 - d * r)
    return r * (2.0 - d * r)


def factor(block, pause):
    shape = (STRIP, BLOCK)
    lane = lax.broadcasted_iota(jnp.int32, shape, 1)
    sub = lax.broadcasted_iota(jnp.int32, shape, 0)
    count = BLOCK // STRIP
    strips = [block[STRIP * t : STRIP * (t + 1), :] for t in range(count)]
    out = []
    for s in range(count):
        if s in (4, 8, 12):
            pause()
        first = STRIP * s
        w = strips[s]
        columns = [jnp.broadcast_to(w[:, first + j : first + j + 1], shape) for j in range(STRIP)]
        a = [[jnp.broadcast_to(columns[j][i : i + 1, :], shape) for j in range(i + 1)] for i in range(STRIP)]
        pivots = jnp.ones(shape, jnp.float32)
        for k in range(STRIP):
            here = lane == first + k
            inverse = recip(a[k][k])
            pivots = jnp.where(sub == k, a[k][k], pivots)
            ratio = {i: a[i][k] * inverse for i in range(k + 1, STRIP)}
            for i in range(k + 1, STRIP):
                for j in range(k + 1, i + 1):
                    a[i][j] = a[i][j] - ratio[i] * a[j][k]
            times = jnp.zeros(shape, jnp.float32)
            for i in range(k + 1, STRIP):
                times = jnp.where(sub == i, ratio[i], times)
            w = jnp.where(here & (sub >= k), jnp.where(sub == k, 1.0, 0.0), w)
            w = w - times * jnp.broadcast_to(w[k : k + 1, :], shape)
        r = w * lax.rsqrt(pivots)
        r = jnp.where((lane > first + sub) & (lane < first + STRIP), 0.0, r)
        out.append(jnp.where(lane <= sub + first, r, 0.0))
        inside = (lane >= first) & (lane < first + STRIP)
        turned = jnp.transpose(r)
        rows = [jnp.broadcast_to(r[i : i + 1, :], shape) for i in range(STRIP)]
        for t in range(s + 1, count):
            total = jnp.where(inside, 0.0, strips[t])
            for i in range(STRIP):
                total = total - jnp.broadcast_to(turned[STRIP * t : STRIP * (t + 1), i : i + 1], shape) * rows[i]
            strips[t] = total
    return jnp.concatenate(out, axis=0)


def split(x):
    high = x.astype(jnp.bfloat16)
    return high, (x - high.astype(jnp.float32)).astype(jnp.bfloat16)


def dot3(ah, al, bh, bl, ca, cb):
    def one(a, b):
        dims = (((ca,), (cb,)), ((), ()))
        return lax.dot_general(a, b, dims, preferred_element_type=jnp.float32)

    return one(ah, bh) + (one(ah, bl) + one(al, bh))


class Net:
    def __init__(self, send_sem, recv_sem):
        self.send_sem, self.recv_sem, self.made, self.open = send_sem, recv_sem, {}, []
        self.index, self.dry = {}, False
        fsdp, tp = lax.axis_index("fsdp"), lax.axis_index("tp")
        self.y, self.z = fsdp // 4, fsdp % 4
        self.x, self.core = tp // 2, tp % 2

    def at(self, y=0, z=0, x=0, core=0):
        f = ((self.y + y + 4) % 4) * 4 + (self.z + z + 4) % 4
        t = ((self.x + x + 4) % 4) * 2 + (self.core + core) % 2
        return (f, t)

    def send(self, key, source, target, to):
        i = self.index.setdefault(key, len(self.index))

        def make():
            return pltpu.make_async_remote_copy(
                src_ref=source(),
                dst_ref=target(),
                send_sem=self.send_sem.at[i],
                recv_sem=self.recv_sem.at[i],
                device_id=self.at(**to),
                device_id_type=MESH,
            )

        self.made[key] = make
        if not self.dry:
            self.open.append(key)
            make().start()

    def got(self, *keys):
        for key in () if self.dry else keys:
            self.made[key]().wait_recv()

    def sent(self, name=None):
        done = [key for key in self.open if name is None or key[0] == name]
        for key in done:
            self.made[key]().wait_send()
        self.open = [key for key in self.open if key not in done]


def shard_of(net, ref, first, o1, o2, half, part):
    dy, dz = (o1, o2) if first == "y" else (o2, o1)
    index = ((net.y + dy + 4) % 4) * 4 + (net.z + dz + 4) % 4
    at, rows = {"all": (0, SHARD), "top": (0, HALF), "low": (HALF, HALF)}[part]
    return ref.at[pl.ds(pl.multiple_of(index * SHARD + at, 8), rows), pl.ds(half * WIDE, WIDE)]


def gather_events(net, name, own, buf):
    lists = []
    for half, (d1, d2) in enumerate((("y", "z"), ("z", "y"))):
        key = lambda *k, half=half: (name, half) + k
        shard = lambda o1, o2, part="all", d1=d1, half=half: shard_of(net, buf, d1, o1, o2, half, part)

        def both(o, key=key, shard=shard, d2=d2):
            for way, sign in ((1, "+"), (-1, "-")):
                net.send(key(2, o, sign), lambda: shard(o, 0), lambda: shard(o, 0), {d2: way})

        def start(key=key, shard=shard, d1=d1, d2=d2, half=half):
            mine = lambda: own(half)
            for way, sign in ((1, "+"), (-1, "-")):
                net.send(key(1, sign), mine, lambda: shard(0, 0), {d1: way})
            for way, sign in ((1, "+"), (-1, "-")):
                net.send(key(2, 0, sign), mine, lambda: shard(0, 0), {d2: way})

        def near(o, way, sign, part, key=key, shard=shard, d1=d1, both=both):
            net.got(key(1, sign))
            net.send(key(1, "f" + sign), lambda: shard(o, 0, part), lambda: shard(o, 0, part), {d1: way})
            both(o)

        def far(key=key, both=both):
            net.got(key(1, "f+"), key(1, "f-"))
            both(2)

        def pass_on(o, p, way, sign, part, key=key, shard=shard, d2=d2):
            net.got(key(2, o, sign))
            net.send(key(2, o, "f" + sign), lambda: shard(o, p, part), lambda: shard(o, p, part), {d2: way})

        def last(key=key):
            for o in (0, -1, 1, 2):
                net.got(key(2, o, "f+"), key(2, o, "f-"))

        events = [start, functools.partial(near, -1, 1, "+", "top"), functools.partial(near, 1, -1, "-", "low")]
        for i, o in enumerate((0, -1, 1, 2)):
            if i == 1:
                events.append(far)
            events.append(functools.partial(pass_on, o, -1, 1, "+", "top"))
            events.append(functools.partial(pass_on, o, 1, -1, "-", "low"))
        events.append(last)
        lists.append(events)
    return [e for pair in zip(*lists) for e in pair]


def scatter_events(net, name, buf, ra, rb, rc, rd):
    lists = []
    order = (2, 1, -1, 0)
    for half, (e1, e2) in enumerate((("y", "z"), ("z", "y"))):
        key = lambda *k, half=half: (name, half) + k
        shard = lambda o1, o2, part="all", e1=e1, half=half: shard_of(net, buf, e1, o1, o2, half, part)

        def add(ref, *others):
            if net.dry:
                return
            total = ref[...]
            for other in others:
                total = total + other[...]
            ref[...] = total

        def start(o, key=key, shard=shard, e1=e1, half=half):
            i = (half * 4 + order.index(o)) * 2
            net.send(key(1, o, "f+"), lambda: shard(2, o, "top"), lambda: ra.at[i], {e1: 1})
            net.send(key(1, o, "f-"), lambda: shard(2, o, "low"), lambda: ra.at[i + 1], {e1: -1})

        def near(o, way, sign, part, j, key=key, shard=shard, e1=e1, half=half):
            i = (half * 4 + order.index(o)) * 2 + j
            net.got(key(1, o, "f" + sign))
            add(shard(way, o, part), ra.at[i])
            net.send(key(1, o, sign), lambda: shard(way, o), lambda: rb.at[i], {e1: way})

        def line(o, key=key, shard=shard, half=half):
            i = (half * 4 + order.index(o)) * 2
            net.got(key(1, o, "+"), key(1, o, "-"))
            add(shard(0, o), rb.at[i], rb.at[i + 1])

        def far(key=key, shard=shard, e2=e2, half=half, line=line):
            line(2)
            net.send(key(2, "f+"), lambda: shard(0, 2, "top"), lambda: rc.at[2 * half], {e2: 1})
            net.send(key(2, "f-"), lambda: shard(0, 2, "low"), lambda: rc.at[2 * half + 1], {e2: -1})

        def side(way, sign, part, j, key=key, shard=shard, e2=e2, half=half, line=line):
            line(way)
            net.got(key(2, "f" + sign))
            add(shard(0, way, part), rc.at[2 * half + j])
            net.send(key(2, sign), lambda: shard(0, way), lambda: rd.at[2 * half + j], {e2: way})

        def mine(key=key, shard=shard, half=half, line=line):
            line(0)
            net.got(key(2, "+"), key(2, "-"))
            add(shard(0, 0), rd.at[2 * half], rd.at[2 * half + 1])

        events = [functools.partial(start, o) for o in order]
        for o in order:
            events.append(functools.partial(near, o, 1, "+", "top", 0))
            events.append(functools.partial(near, o, -1, "-", "low", 1))
            if o == 1:
                events.append(far)
        events.append(functools.partial(side, 1, "+", "top", 0))
        events.append(functools.partial(side, -1, "-", "low", 1))
        events.append(mine)
        lists.append(events)
    return [e for pair in zip(*lists) for e in pair]


def tp_gather_events(net, name, ref, piece, start_of):
    def part(dx, which="all"):
        at, rows = {"all": (0, piece), "top": (0, piece // 2), "low": (piece // 2, piece // 2)}[which]
        return ref.at[pl.ds(pl.multiple_of(start_of(dx) + at, 8), rows), :]

    def put(key, dx, which, to):
        net.send((name,) + key, lambda: part(dx, which), lambda: part(dx, which), to)

    def start():
        put(("+",), 0, "all", {"x": 1})
        put(("-",), 0, "all", {"x": -1})
        put(("c", 0), 0, "all", {"core": 1})

    def near():
        net.got((name, "+"))
        put(("f+",), -1, "top", {"x": 1})
        net.got((name, "-"))
        put(("f-",), 1, "low", {"x": -1})
        put(("c", -1), -1, "all", {"core": 1})
        put(("c", 1), 1, "all", {"core": 1})

    def last():
        net.got((name, "f+"), (name, "f-"))
        put(("c", 2), 2, "all", {"core": 1})
        net.got(*[(name, "c", dx) for dx in (0, -1, 1, 2)])

    return start, near, last


def tp_sum(net, ref, out, lc, la, lb):
    mine = net.core * 256
    other = 256 - mine
    net.send(("core",), lambda: ref.at[pl.ds(pl.multiple_of(other, 8), 256), :], lambda: lc, {"core": 1})
    net.got(("core",))
    rows = pl.ds(pl.multiple_of(mine, 8), 256)
    ref[rows, :] = ref[rows, :] + lc[...]

    def start_of(dx):
        return mine + ((net.x + dx + 4) % 4) * 64

    def piece(dx, at=0, count=64):
        return ref.at[pl.ds(pl.multiple_of(start_of(dx) + at, 8), count), :]

    net.send(("xf+",), lambda: piece(2, 0, 32), lambda: la.at[0], {"x": 1})
    net.send(("xf-",), lambda: piece(2, 32, 32), lambda: la.at[1], {"x": -1})
    for way, sign, at, j in ((1, "+", 0, 0), (-1, "-", 32, 1)):
        net.got(("xf" + sign,))
        there = piece(way, at, 32)
        there[...] = there[...] + la[j]
        net.send(("x" + sign,), lambda way=way: piece(way), lambda j=j: lb.at[j], {"x": way})
    net.got(("x+",), ("x-",))
    out[pl.ds(pl.multiple_of(start_of(0), 8), 64), :] = piece(0)[...] + lb[0] + lb[1]
    for event in tp_gather_events(net, "left", out, 64, start_of):
        event()


def main_kernel(
    momentum_ref, gradient_ref, basis_ref, rh, rl, oh, sh, sl, basis_out,
    momentum_in, gradient_in, in_sem, left_ref, cross_ref, ih, il, sq, buf, mh, ml, lbuf, lc, la, lb, lh, ll, ra, rb, rc, rd, held, gpart, gsum, send_sem, recv_sem,
):
    net = Net(send_sem, recv_sem)
    me = net.y * 4 + net.z
    tp = net.x * 2 + net.core
    barrier = pltpu.get_barrier_semaphore()
    for i in range(1, 16):
        pl.semaphore_signal(barrier, inc=1, device_id=((me + i) % 16, tp), device_id_type=MESH)
    for i in range(1, 8):
        pl.semaphore_signal(barrier, inc=1, device_id=(me, (tp + i) % 8), device_id_type=MESH)
    pl.semaphore_wait(barrier, 15 + 7)

    events = gather_events(net, "basis", lambda half: basis_ref.at[:, pl.ds(half * WIDE, WIDE)], buf)
    for event in events[:2]:
        event()
    buf[pl.ds(pl.multiple_of(me * SHARD, 8), SHARD), :] = basis_ref[...]

    def load(i, slot):
        rows = pl.ds(pl.multiple_of(i * 64, 64), 64)
        return (
            pltpu.make_async_copy(momentum_ref.at[rows, :], momentum_in.at[slot], in_sem.at[0, slot]),
            pltpu.make_async_copy(gradient_ref.at[rows, :], gradient_in.at[slot], in_sem.at[1, slot]),
        )

    for i in range(8):
        if i == 0:
            for copy in load(0, 0):
                copy.start()
        if i < 7:
            for copy in load(i + 1, (i + 1) % 2):
                copy.start()
        for copy in load(i, i % 2):
            copy.wait()
        rows = slice(64 * i, 64 * i + 64)
        mh[rows, :], ml[rows, :] = split(momentum_in[i % 2] + gradient_in[i % 2].astype(jnp.float32))

    for event in events[2:]:
        event()

    @pl.loop(0, 4)
    def _(i):
        columns = pl.ds(pl.multiple_of(i * 256, 256), 256)
        bh, bl = split(buf[:, columns])
        lbuf[:, columns] = dot3(mh[...], ml[...], bh, bl, 1, 0)

    tp_sum(net, lbuf, left_ref, lc, la, lb)
    net.sent()

    own_rows = pl.ds(pl.multiple_of(tp * BLOCK, BLOCK), BLOCK)
    gpart[...] = dot(left_ref[:, own_rows], left_ref[...], 0, 0, HIGHEST)
    copies = []
    for i in range(1, 16):
        to = (me + i) % 16
        copies.append(
            pltpu.make_async_remote_copy(
                src_ref=gpart.at[pl.ds(pl.multiple_of(to * 8, 8), 8), :],
                dst_ref=gsum.at[i],
                send_sem=send_sem.at[150 + i],
                recv_sem=recv_sem.at[150 + i],
                device_id=(to, tp),
                device_id_type=MESH,
            )
        )
        copies[-1].start()

    lh[...], ll[...] = split(left_ref[...])

    @pl.loop(0, 7)
    def _(i):
        columns = pl.ds(pl.multiple_of(i * 256, 256), 256)
        buf[columns, :] = dot3(mh[:, columns], ml[:, columns], lh[...], ll[...], 0, 0)

    scatter = scatter_events(net, "scatter", buf, ra, rb, rc, rd)
    for copy in copies:
        copy.wait()
    total = gpart[pl.ds(pl.multiple_of(me * 8, 8), 8), :]
    for i in range(1, 16):
        total = total + gsum[i]
    at = pl.multiple_of(tp * BLOCK + me * 8, 8)
    held[pl.ds(at, 8), :] = total
    copies = []
    for i in range(1, 16):
        copies.append(
            pltpu.make_async_remote_copy(
                src_ref=held.at[pl.ds(at, 8), :],
                dst_ref=held.at[pl.ds(at, 8), :],
                send_sem=send_sem.at[170 + i],
                recv_sem=recv_sem.at[170 + i],
                device_id=((me + i) % 16, tp),
                device_id_type=MESH,
            )
        )
        copies[-1].start()
    for event in scatter[:12]:
        event()
    for copy in copies:
        copy.wait()
    gram_events = tp_gather_events(
        net, "gram", held, BLOCK, lambda dx: (((net.x + dx + 4) % 4) * 2 + net.core) * BLOCK
    )
    gram_events[0]()
    for event in scatter[12:18]:
        event()
    gram_events[1]()
    for event in scatter[18:22]:
        event()
    gram_events[2]()
    net.sent("gram")

    def own(half):
        return shard_of(net, buf, "y", 0, 0, half, "all")

    def keep():
        if net.dry:
            return
        rows = pl.ds(pl.multiple_of(me * SHARD, 8), SHARD)
        cross_ref[rows, :] = buf[rows, :]

    rest = scatter[22:] + [keep] + gather_events(net, "cross", own, cross_ref)
    eliminate(net, held, ih, il, rest)
    net.sent()

    sq[0] = jnp.zeros((8, RANK), jnp.float32)

    @pl.loop(0, 7)
    def _(i):
        rows = pl.ds(pl.multiple_of(i * 256, 256), 256)
        wh, wl = split(cross_ref[rows, :])
        for n in range(4):
            upto = 256 * (n + 1)
            block = slice(256 * n, upto)
            part = dot3(wh[:, :upto], wl[:, :upto], ih[block, :upto], il[block, :upto], 1, 1)
            rh[rows, block], rl[rows, block] = split(part)
            sq[0, :, block] = sq[0, :, block] + jnp.sum((part * part).reshape(32, 8, 256), axis=0)

    copies = []
    for i in range(1, 8):
        copies.append(
            pltpu.make_async_remote_copy(
                src_ref=sq.at[0],
                dst_ref=sq.at[i],
                send_sem=send_sem.at[190 + i],
                recv_sem=recv_sem.at[190 + i],
                device_id=(me, (tp + i) % 8),
                device_id_type=MESH,
            )
        )
        copies[-1].start()
    for n in range(4):
        upto = 256 * (n + 1)
        block = slice(256 * n, upto)
        lbuf[:, block] = dot3(lh[:, :upto], ll[:, :upto], ih[block, :upto], il[block, :upto], 1, 1)
    oh[...] = (0.05 * lbuf[...]).astype(jnp.bfloat16)
    for copy in copies:
        copy.wait()
    total = sq[0]
    for i in range(1, 8):
        total = total + sq[i]
    over = 1.0 / jnp.sqrt(jnp.sum(total, axis=0, keepdims=True) + 1e-08)
    scale = jnp.sqrt(jnp.float32(M) * jnp.float32(N) / jnp.float32(RANK))
    sh[...], sl[...] = split(lbuf[...] * (scale * over))
    rows = pl.ds(pl.multiple_of(me * SHARD, 16), SHARD)
    basis_out[...] = (rh[rows, :].astype(jnp.float32) + rl[rows, :].astype(jnp.float32)) * over


def eliminate(net, held, ih, il, events):
    n = held.shape[0]
    count = n // BLOCK
    shape = (BLOCK, BLOCK)
    eye = (lax.broadcasted_iota(jnp.int32, shape, 0) == lax.broadcasted_iota(jnp.int32, shape, 1)).astype(jnp.float32)
    lanes = lax.broadcasted_iota(jnp.int32, (BLOCK, n), 1)
    slots = 5 * count
    plan = [events[len(events) * i // slots : len(events) * (i + 1) // slots] for i in range(slots)]
    net.dry = True
    for event in events:
        event()
    net.dry = False

    def step(k, carry):
        used = []

        def pause():
            for i in range(count):
                group = plan[5 * i + len(used)]
                if group:

                    @pl.when(k == i)
                    def _():
                        for event in group:
                            event()

            used.append(None)

        mine = pl.ds(pl.multiple_of(k * BLOCK, BLOCK), BLOCK)
        pause()
        inverse = factor(held[mine, mine], pause)
        held[mine, mine] = eye
        held[mine, :] = dot(inverse, held[mine, :], 1, 0, HIGHEST)
        ih[mine, :], il[mine, :] = split(jnp.where(lanes < (k + 1) * BLOCK, held[mine, :], 0.0))
        pause()

        def below(t, inner):
            rows = pl.ds(pl.multiple_of(t * BLOCK, BLOCK), BLOCK)
            held[rows, mine] = jnp.zeros(shape, jnp.float32)
            held[rows, :] = held[rows, :] - dot(held[mine, rows], held[mine, :], 0, 0, HIGHEST)
            return inner

        lax.fori_loop(k + 1, count, below, 0)
        return carry

    lax.fori_loop(0, count, step, 0)


def factors(momentum, gradient, basis):
    f32, bf16 = jnp.float32, jnp.bfloat16
    rows, columns = momentum.shape
    vmem = pl.BlockSpec(memory_space=pltpu.VMEM)
    return pl.pallas_call(
        main_kernel,
        out_shape=[
            jax.ShapeDtypeStruct((columns, RANK), bf16),
            jax.ShapeDtypeStruct((columns, RANK), bf16),
            jax.ShapeDtypeStruct((rows, RANK), bf16),
            jax.ShapeDtypeStruct((rows, RANK), bf16),
            jax.ShapeDtypeStruct((rows, RANK), bf16),
            jax.ShapeDtypeStruct((SHARD, RANK), f32),
        ],
        in_specs=[pl.BlockSpec(memory_space=pl.ANY)] * 2 + [vmem],
        out_specs=[vmem] * 6,
        scratch_shapes=[
            pltpu.VMEM((2, 64, columns), f32),
            pltpu.VMEM((2, 64, columns), bf16),
            pltpu.SemaphoreType.DMA((2, 2)),
            pltpu.VMEM((rows, RANK), f32),
            pltpu.VMEM((columns, RANK), f32),
            pltpu.VMEM((RANK, RANK), bf16),
            pltpu.VMEM((RANK, RANK), bf16),
            pltpu.VMEM((8, 8, RANK), f32),
            pltpu.VMEM((columns, RANK), f32),
            pltpu.VMEM((rows, columns), bf16),
            pltpu.VMEM((rows, columns), bf16),
            pltpu.VMEM((rows, RANK), f32),
            pltpu.VMEM((256, RANK), f32),
            pltpu.VMEM((2, 32, RANK), f32),
            pltpu.VMEM((2, 64, RANK), f32),
            pltpu.VMEM((rows, RANK), bf16),
            pltpu.VMEM((rows, RANK), bf16),
            pltpu.VMEM((16, HALF, WIDE), f32),
            pltpu.VMEM((16, SHARD, WIDE), f32),
            pltpu.VMEM((4, HALF, WIDE), f32),
            pltpu.VMEM((4, SHARD, WIDE), f32),
            pltpu.VMEM((RANK, RANK), f32),
            pltpu.VMEM((BLOCK, RANK), f32),
            pltpu.VMEM((16, 8, RANK), f32),
            pltpu.SemaphoreType.DMA((200,)),
            pltpu.SemaphoreType.DMA((200,)),
        ],
        compiler_params=pltpu.CompilerParams(
            collective_id=0, has_side_effects=True, vmem_limit_bytes=63 << 20
        ),
        cost_estimate=pl.CostEstimate(flops=60_000_000_000, bytes_accessed=30 << 20, transcendentals=0),
        name="factors",
    )(momentum, gradient, basis)


def output_kernel(momentum_ref, gradient_ref, rh_ref, rl_ref, oh_ref, sh_ref, sl_ref, momentum_out, update_out):
    rh, rl = rh_ref[...], rl_ref[...]
    dims = (((1,), (1,)), ((), ()))
    low = lax.dot_general(oh_ref[...], rh, dims, preferred_element_type=jnp.float32)
    momentum_out[...] = (momentum_ref[...] + gradient_ref[...].astype(jnp.float32)) - low
    update_out[...] = dot3(sh_ref[...], sl_ref[...], rh, rl, 1, 1).astype(jnp.bfloat16)


def outputs(momentum, gradient, rh, rl, oh, sh, sl):
    rows, columns = momentum.shape
    wide = 256
    tile = pl.BlockSpec((rows, wide), lambda i: (0, i))
    right = pl.BlockSpec((wide, RANK), lambda i: (i, 0))
    whole = pl.BlockSpec((rows, RANK), lambda i: (0, 0))
    return pl.pallas_call(
        output_kernel,
        grid=(columns // wide,),
        out_shape=[
            jax.ShapeDtypeStruct((rows, columns), jnp.float32),
            jax.ShapeDtypeStruct((rows, columns), jnp.bfloat16),
        ],
        in_specs=[tile, tile, right, right, whole, whole, whole],
        out_specs=[tile, tile],
        compiler_params=pltpu.CompilerParams(vmem_limit_bytes=32 << 20),
        name="outputs",
    )(momentum, gradient, rh, rl, oh, sh, sl)


def local(gradient, momentum, basis):
    rh, rl, oh, sh, sl, new_basis = factors(momentum, gradient, basis)
    new_momentum, update = outputs(momentum, gradient, rh, rl, oh, sh, sl)
    return (new_momentum, new_basis, update)


def solution(mesh):
    placed = (P("fsdp", "tp"), P("fsdp", "tp"), P(("tp", "fsdp"), None))
    return jax.shard_map(
        local,
        mesh=mesh,
        in_specs=placed,
        out_specs=(P("fsdp", "tp"), P(("tp", "fsdp"), None), P("fsdp", "tp")),
        check_vma=False,
    )
```

```python
import functools

import jax
import jax.numpy as jnp
from jax import lax
from jax.experimental import pallas as pl
from jax.experimental.pallas import tpu as pltpu
from jax.sharding import PartitionSpec as P

M = 8192
N = 14336
RANK = 1024
BLOCK = 128
STRIP = 8
HIGHEST = lax.Precision.HIGHEST
HIGH = lax.Precision.HIGH
MESH = pl.DeviceIdType.MESH
SHARD = 112
HALF = 56
WIDE = 512


def dot(a, b, ca, cb, precision):
    dims = (((ca,), (cb,)), ((), ()))
    return lax.dot_general(a, b, dims, precision=precision, preferred_element_type=jnp.float32)


def recip(d):
    r = pl.reciprocal(d, approx=True)
    r = r * (2.0 - d * r)
    return r * (2.0 - d * r)


def factor(block, pause):
    shape = (STRIP, BLOCK)
    lane = lax.broadcasted_iota(jnp.int32, shape, 1)
    sub = lax.broadcasted_iota(jnp.int32, shape, 0)
    count = BLOCK // STRIP
    strips = [block[STRIP * t : STRIP * (t + 1), :] for t in range(count)]
    out = []
    for s in range(count):
        if s in (4, 8, 12):
            pause()
        first = STRIP * s
        w = strips[s]
        columns = [jnp.broadcast_to(w[:, first + j : first + j + 1], shape) for j in range(STRIP)]
        a = [[jnp.broadcast_to(columns[j][i : i + 1, :], shape) for j in range(i + 1)] for i in range(STRIP)]
        pivots = jnp.ones(shape, jnp.float32)
        for k in range(STRIP):
            here = lane == first + k
            inverse = recip(a[k][k])
            pivots = jnp.where(sub == k, a[k][k], pivots)
            ratio = {i: a[i][k] * inverse for i in range(k + 1, STRIP)}
            for i in range(k + 1, STRIP):
                for j in range(k + 1, i + 1):
                    a[i][j] = a[i][j] - ratio[i] * a[j][k]
            times = jnp.zeros(shape, jnp.float32)
            for i in range(k + 1, STRIP):
                times = jnp.where(sub == i, ratio[i], times)
            w = jnp.where(here & (sub >= k), jnp.where(sub == k, 1.0, 0.0), w)
            w = w - times * jnp.broadcast_to(w[k : k + 1, :], shape)
        r = w * lax.rsqrt(pivots)
        r = jnp.where((lane > first + sub) & (lane < first + STRIP), 0.0, r)
        out.append(jnp.where(lane <= sub + first, r, 0.0))
        inside = (lane >= first) & (lane < first + STRIP)
        turned = jnp.transpose(r)
        rows = [jnp.broadcast_to(r[i : i + 1, :], shape) for i in range(STRIP)]
        for t in range(s + 1, count):
            total = jnp.where(inside, 0.0, strips[t])
            for i in range(STRIP):
                total = total - jnp.broadcast_to(turned[STRIP * t : STRIP * (t + 1), i : i + 1], shape) * rows[i]
            strips[t] = total
    return jnp.concatenate(out, axis=0)


def split(x):
    high = x.astype(jnp.bfloat16)
    return high, (x - high.astype(jnp.float32)).astype(jnp.bfloat16)


def dot3(ah, al, bh, bl, ca, cb):
    def one(a, b):
        dims = (((ca,), (cb,)), ((), ()))
        return lax.dot_general(a, b, dims, preferred_element_type=jnp.float32)

    return one(ah, bh) + (one(ah, bl) + one(al, bh))


class Net:
    def __init__(self, send_sem, recv_sem):
        self.send_sem, self.recv_sem, self.made, self.open = send_sem, recv_sem, {}, []
        self.index, self.dry = {}, False
        fsdp, tp = lax.axis_index("fsdp"), lax.axis_index("tp")
        self.y, self.z = fsdp // 4, fsdp % 4
        self.x, self.core = tp // 2, tp % 2

    def at(self, y=0, z=0, x=0, core=0):
        f = ((self.y + y + 4) % 4) * 4 + (self.z + z + 4) % 4
        t = ((self.x + x + 4) % 4) * 2 + (self.core + core) % 2
        return (f, t)

    def send(self, key, source, target, to):
        i = self.index.setdefault(key, len(self.index))

        def make():
            return pltpu.make_async_remote_copy(
                src_ref=source(),
                dst_ref=target(),
                send_sem=self.send_sem.at[i],
                recv_sem=self.recv_sem.at[i],
                device_id=self.at(**to),
                device_id_type=MESH,
            )

        self.made[key] = make
        if not self.dry:
            self.open.append(key)
            make().start()

    def got(self, *keys):
        for key in () if self.dry else keys:
            self.made[key]().wait_recv()

    def sent(self, name=None):
        done = [key for key in self.open if name is None or key[0] == name]
        for key in done:
            self.made[key]().wait_send()
        self.open = [key for key in self.open if key not in done]


def shard_of(net, ref, first, o1, o2, columns, part):
    dy, dz = (o1, o2) if first == "y" else (o2, o1)
    index = ((net.y + dy + 4) % 4) * 4 + (net.z + dz + 4) % 4
    at, rows = {"all": (0, SHARD), "top": (0, HALF), "low": (HALF, HALF)}[part]
    return ref.at[pl.ds(pl.multiple_of(index * SHARD + at, 8), rows), columns]


def both_lists(one, other):
    order = [((i + 0.5) / len(one), 0, i) for i in range(len(one))]
    order += [((i + 0.5) / len(other), 1, i) for i in range(len(other))]
    return [(one, other)[which][i] for _, which, i in sorted(order)]


def gather_events(net, name, own, buf, d1, d2, columns):
    def key(*k):
        return (name, d1) + k

    def shard(o1, o2, part="all"):
        return shard_of(net, buf, d1, o1, o2, columns, part)

    def both(o):
        for way, sign in ((1, "+"), (-1, "-")):
            net.send(key(2, o, sign), lambda: shard(o, 0), lambda: shard(o, 0), {d2: way})

    def start():
        for way, sign in ((1, "+"), (-1, "-")):
            net.send(key(1, sign), own, lambda: shard(0, 0), {d1: way})
        for way, sign in ((1, "+"), (-1, "-")):
            net.send(key(2, 0, sign), own, lambda: shard(0, 0), {d2: way})

    def near(o, way, sign, part):
        net.got(key(1, sign))
        net.send(key(1, "f" + sign), lambda: shard(o, 0, part), lambda: shard(o, 0, part), {d1: way})
        both(o)

    def far():
        net.got(key(1, "f+"), key(1, "f-"))
        both(2)

    def pass_on(o, p, way, sign, part):
        net.got(key(2, o, sign))
        net.send(key(2, o, "f" + sign), lambda: shard(o, p, part), lambda: shard(o, p, part), {d2: way})

    def last():
        for o in (0, -1, 1, 2):
            net.got(key(2, o, "f+"), key(2, o, "f-"))

    events = [start, functools.partial(near, -1, 1, "+", "top"), functools.partial(near, 1, -1, "-", "low")]
    for i, o in enumerate((0, -1, 1, 2)):
        if i == 1:
            events.append(far)
        events.append(functools.partial(pass_on, o, -1, 1, "+", "top"))
        events.append(functools.partial(pass_on, o, 1, -1, "-", "low"))
    events.append(last)
    return events


def scatter_events(net, name, buf, ra, rb, rc, rd, e1, e2, half):
    order = (2, 1, -1, 0)
    columns = pl.ds(half * WIDE, WIDE)

    def key(*k):
        return (name, e1) + k

    def shard(o1, o2, part="all"):
        return shard_of(net, buf, e1, o1, o2, columns, part)

    def slot(o):
        return (half * 4 + order.index(o)) * 2

    def add(ref, *others):
        if net.dry:
            return
        total = ref[...]
        for other in others:
            total = total + other[...]
        ref[...] = total

    def start(o):
        net.send(key(1, o, "f+"), lambda: shard(2, o, "top"), lambda: ra.at[slot(o)], {e1: 1})
        net.send(key(1, o, "f-"), lambda: shard(2, o, "low"), lambda: ra.at[slot(o) + 1], {e1: -1})

    def near(o, way, sign, part, j):
        net.got(key(1, o, "f" + sign))
        add(shard(way, o, part), ra.at[slot(o) + j])
        net.send(key(1, o, sign), lambda: shard(way, o), lambda: rb.at[slot(o) + j], {e1: way})

    def line(o):
        net.got(key(1, o, "+"), key(1, o, "-"))
        add(shard(0, o), rb.at[slot(o)], rb.at[slot(o) + 1])

    def far():
        line(2)
        net.send(key(2, "f+"), lambda: shard(0, 2, "top"), lambda: rc.at[2 * half], {e2: 1})
        net.send(key(2, "f-"), lambda: shard(0, 2, "low"), lambda: rc.at[2 * half + 1], {e2: -1})

    def side(way, sign, part, j):
        line(way)
        net.got(key(2, "f" + sign))
        add(shard(0, way, part), rc.at[2 * half + j])
        net.send(key(2, sign), lambda: shard(0, way), lambda: rd.at[2 * half + j], {e2: way})

    def mine():
        line(0)
        net.got(key(2, "+"), key(2, "-"))
        add(shard(0, 0), rd.at[2 * half], rd.at[2 * half + 1])

    events = [functools.partial(start, o) for o in order]
    for o in order:
        events.append(functools.partial(near, o, 1, "+", "top", 0))
        events.append(functools.partial(near, o, -1, "-", "low", 1))
        if o == 1:
            events.append(far)
    events.append(functools.partial(side, 1, "+", "top", 0))
    events.append(functools.partial(side, -1, "-", "low", 1))
    events.append(mine)
    return events


def tp_gather_events(net, name, ref, piece, start_of, columns=slice(None)):
    def part(dx, which="all"):
        at, rows = {"all": (0, piece), "top": (0, piece // 2), "low": (piece // 2, piece // 2)}[which]
        return ref.at[pl.ds(pl.multiple_of(start_of(dx) + at, 8), rows), columns]

    def put(key, dx, which, to):
        net.send((name,) + key, lambda: part(dx, which), lambda: part(dx, which), to)

    def start():
        put(("+",), 0, "all", {"x": 1})
        put(("-",), 0, "all", {"x": -1})
        put(("c", 0), 0, "all", {"core": 1})

    def near():
        net.got((name, "+"))
        put(("f+",), -1, "top", {"x": 1})
        net.got((name, "-"))
        put(("f-",), 1, "low", {"x": -1})
        put(("c", -1), -1, "all", {"core": 1})
        put(("c", 1), 1, "all", {"core": 1})

    def last():
        net.got((name, "f+"), (name, "f-"))
        put(("c", 2), 2, "all", {"core": 1})
        net.got(*[(name, "c", dx) for dx in (0, -1, 1, 2)])

    return start, near, last


def tp_sum_events(net, ref, out, lc, la, lb, half):
    mine = net.core * 256
    columns = pl.ds(half * WIDE, WIDE)

    def key(k):
        return ("sum", half, k)

    def rows_at(at, count, of=ref):
        return of.at[pl.ds(pl.multiple_of(at, 8), count), columns]

    def start_of(dx):
        return mine + ((net.x + dx + 4) % 4) * 64

    def piece(dx, at=0, count=64):
        return rows_at(start_of(dx) + at, count)

    def start():
        net.send(key("core"), lambda: rows_at(256 - mine, 256), lambda: lc.at[half], {"core": 1})

    def pair():
        net.got(key("core"))
        there = rows_at(mine, 256)
        there[...] = there[...] + lc[half]
        net.send(key("f+"), lambda: piece(2, 0, 32), lambda: la.at[half, 0], {"x": 1})
        net.send(key("f-"), lambda: piece(2, 32, 32), lambda: la.at[half, 1], {"x": -1})

    def side():
        for way, sign, at, j in ((1, "+", 0, 0), (-1, "-", 32, 1)):
            net.got(key("f" + sign))
            there = piece(way, at, 32)
            there[...] = there[...] + la[half, j]
            net.send(key(sign), lambda way=way: piece(way), lambda j=j: lb.at[half, j], {"x": way})

    gather = tp_gather_events(net, "left%d" % half, out, 64, start_of, columns)

    def own():
        net.got(key("+"), key("-"))
        there = rows_at(start_of(0), 64, out)
        there[...] = piece(0)[...] + lb[half, 0] + lb[half, 1]
        gather[0]()

    return [start, pair, side, own, gather[1], gather[2]]


def main_kernel(
    momentum_ref, gradient_ref, basis_ref, rh, rl, oh, sh, sl, basis_out,
    momentum_in, gradient_in, in_sem, left_ref, cross_ref, ih, il, sq, buf, mh, ml, lbuf, lc, la, lb, lh, ll, ra, rb, rc, rd, held, gpart, gsum, send_sem, recv_sem,
):
    net = Net(send_sem, recv_sem)
    me = net.y * 4 + net.z
    tp = net.x * 2 + net.core
    barrier = pltpu.get_barrier_semaphore()
    for i in range(1, 16):
        pl.semaphore_signal(barrier, inc=1, device_id=((me + i) % 16, tp), device_id_type=MESH)
    for i in range(1, 8):
        pl.semaphore_signal(barrier, inc=1, device_id=(me, (tp + i) % 8), device_id_type=MESH)
    pl.semaphore_wait(barrier, 15 + 7)

    def run(events):
        for event in events:
            event()

    gathers = []
    for half in range(2):
        lists = []
        for i, axes in enumerate((("y", "z"), ("z", "y"))):
            columns = pl.ds(half * WIDE + i * 256, 256)
            lists.append(gather_events(net, "basis%d" % half, lambda c=columns: basis_ref.at[:, c], buf, *axes, columns))
        gathers.append(both_lists(*lists))
    g0, g1 = gathers
    run(g0[:2])
    buf[pl.ds(pl.multiple_of(me * SHARD, 8), SHARD), :] = basis_ref[...]

    def load(i, slot):
        rows = pl.ds(pl.multiple_of(i * 64, 64), 64)
        return (
            pltpu.make_async_copy(momentum_ref.at[rows, :], momentum_in.at[slot], in_sem.at[0, slot]),
            pltpu.make_async_copy(gradient_ref.at[rows, :], gradient_in.at[slot], in_sem.at[1, slot]),
        )

    for i in range(8):
        if i == 0:
            for copy in load(0, 0):
                copy.start()
        if i < 7:
            for copy in load(i + 1, (i + 1) % 2):
                copy.start()
        for copy in load(i, i % 2):
            copy.wait()
        rows = slice(64 * i, 64 * i + 64)
        mh[rows, :], ml[rows, :] = split(momentum_in[i % 2] + gradient_in[i % 2].astype(jnp.float32))

    def left_part(half):
        @pl.loop(0, 2)
        def _(i):
            columns = pl.ds(pl.multiple_of(half * WIDE + i * 256, 256), 256)
            bh, bl = split(buf[:, columns])
            lbuf[:, columns] = dot3(mh[...], ml[...], bh, bl, 1, 0)

    def cross_part(half):
        half_columns = slice(half * WIDE, (half + 1) * WIDE)
        lh[:, half_columns], ll[:, half_columns] = split(left_ref[:, half_columns])
        net.sent("basis%d" % half)

        @pl.loop(0, 7)
        def _(i):
            columns = pl.ds(pl.multiple_of(i * 256, 256), 256)
            buf[columns, half_columns] = dot3(
                mh[:, columns], ml[:, columns], lh[:, half_columns], ll[:, half_columns], 0, 0
            )

    t0, t1 = [tp_sum_events(net, lbuf, left_ref, lc, la, lb, half) for half in range(2)]
    s0 = scatter_events(net, "scatter", buf, ra, rb, rc, rd, "y", "z", 0)
    s1 = scatter_events(net, "scatter", buf, ra, rb, rc, rd, "z", "y", 1)
    run(g0[2:8] + g1[:2] + g0[8:14] + g1[2:6] + g0[14:20] + g1[6:10] + g0[20:])
    left_part(0)
    run(t0[:1] + g1[10:14] + t0[1:2] + g1[14:16] + t0[2:3] + g1[16:19])
    run(t0[3:4] + g1[19:22] + t0[4:5] + g1[22:24] + t0[5:] + g1[24:])
    left_part(1)
    run(t1[:1])
    cross_part(0)
    run(t1[1:2] + s0[:4] + t1[2:3] + s0[4:6] + t1[3:5] + s0[6:8] + t1[5:])

    own_rows = pl.ds(pl.multiple_of(tp * BLOCK, BLOCK), BLOCK)
    gpart[...] = dot(left_ref[:, own_rows], left_ref[...], 0, 0, HIGHEST)
    copies = []
    for i in range(1, 16):
        to = (me + i) % 16
        copies.append(
            pltpu.make_async_remote_copy(
                src_ref=gpart.at[pl.ds(pl.multiple_of(to * 8, 8), 8), :],
                dst_ref=gsum.at[i],
                send_sem=send_sem.at[220 + i],
                recv_sem=recv_sem.at[220 + i],
                device_id=(to, tp),
                device_id_type=MESH,
            )
        )
        copies[-1].start()

    cross_part(1)
    for copy in copies:
        copy.wait()
    total = gpart[pl.ds(pl.multiple_of(me * 8, 8), 8), :]
    for i in range(1, 16):
        total = total + gsum[i]
    at = pl.multiple_of(tp * BLOCK + me * 8, 8)
    held[pl.ds(at, 8), :] = total
    copies = []
    for i in range(1, 16):
        copies.append(
            pltpu.make_async_remote_copy(
                src_ref=held.at[pl.ds(at, 8), :],
                dst_ref=held.at[pl.ds(at, 8), :],
                send_sem=send_sem.at[236 + i],
                recv_sem=recv_sem.at[236 + i],
                device_id=((me + i) % 16, tp),
                device_id_type=MESH,
            )
        )
        copies[-1].start()
    run(s1[:4] + s0[8:11])
    for copy in copies:
        copy.wait()
    gram_events = tp_gather_events(
        net, "gram", held, BLOCK, lambda dx: (((net.x + dx + 4) % 4) * 2 + net.core) * BLOCK
    )
    gram_events[0]()
    run(s0[11:13] + s1[4:8])
    gram_events[1]()
    run(s0[13:15] + s1[8:11])
    gram_events[2]()
    net.sent("gram")

    rows = pl.ds(pl.multiple_of(me * SHARD, 8), SHARD)

    def keep(columns):
        if not net.dry:
            cross_ref[rows, columns] = buf[rows, columns]

    rest = []
    for half, axes, begun in ((0, ("y", "z"), s0[15:]), (1, ("z", "y"), s1[11:])):
        columns = pl.ds(half * WIDE, WIDE)
        rest.append(begun + [functools.partial(keep, columns)])
        rest[-1] += gather_events(net, "cross", lambda c=columns: buf.at[rows, c], cross_ref, *axes, columns)
    rest = both_lists(*rest)
    eliminate(net, held, ih, il, rest)
    net.sent()

    sq[0] = jnp.zeros((8, RANK), jnp.float32)

    @pl.loop(0, 7)
    def _(i):
        rows = pl.ds(pl.multiple_of(i * 256, 256), 256)
        wh, wl = split(cross_ref[rows, :])
        for n in range(4):
            upto = 256 * (n + 1)
            block = slice(256 * n, upto)
            part = dot3(wh[:, :upto], wl[:, :upto], ih[block, :upto], il[block, :upto], 1, 1)
            rh[rows, block], rl[rows, block] = split(part)
            sq[0, :, block] = sq[0, :, block] + jnp.sum((part * part).reshape(32, 8, 256), axis=0)

    copies = []
    for i in range(1, 8):
        copies.append(
            pltpu.make_async_remote_copy(
                src_ref=sq.at[0],
                dst_ref=sq.at[i],
                send_sem=send_sem.at[252 + i],
                recv_sem=recv_sem.at[252 + i],
                device_id=(me, (tp + i) % 8),
                device_id_type=MESH,
            )
        )
        copies[-1].start()
    for n in range(4):
        upto = 256 * (n + 1)
        block = slice(256 * n, upto)
        lbuf[:, block] = dot3(lh[:, :upto], ll[:, :upto], ih[block, :upto], il[block, :upto], 1, 1)
    oh[...] = (0.05 * lbuf[...]).astype(jnp.bfloat16)
    for copy in copies:
        copy.wait()
    total = sq[0]
    for i in range(1, 8):
        total = total + sq[i]
    over = 1.0 / jnp.sqrt(jnp.sum(total, axis=0, keepdims=True) + 1e-08)
    scale = jnp.sqrt(jnp.float32(M) * jnp.float32(N) / jnp.float32(RANK))
    sh[...], sl[...] = split(lbuf[...] * (scale * over))
    rows = pl.ds(pl.multiple_of(me * SHARD, 16), SHARD)
    basis_out[...] = (rh[rows, :].astype(jnp.float32) + rl[rows, :].astype(jnp.float32)) * over


def eliminate(net, held, ih, il, events):
    n = held.shape[0]
    count = n // BLOCK
    shape = (BLOCK, BLOCK)
    eye = (lax.broadcasted_iota(jnp.int32, shape, 0) == lax.broadcasted_iota(jnp.int32, shape, 1)).astype(jnp.float32)
    lanes = lax.broadcasted_iota(jnp.int32, (BLOCK, n), 1)
    slots = 5 * count
    plan = [events[len(events) * i // slots : len(events) * (i + 1) // slots] for i in range(slots)]
    net.dry = True
    for event in events:
        event()
    net.dry = False

    def step(k, carry):
        used = []

        def pause():
            for i in range(count):
                group = plan[5 * i + len(used)]
                if group:

                    @pl.when(k == i)
                    def _():
                        for event in group:
                            event()

            used.append(None)

        mine = pl.ds(pl.multiple_of(k * BLOCK, BLOCK), BLOCK)
        pause()
        inverse = factor(held[mine, mine], pause)
        held[mine, mine] = eye
        held[mine, :] = dot(inverse, held[mine, :], 1, 0, HIGHEST)
        ih[mine, :], il[mine, :] = split(jnp.where(lanes < (k + 1) * BLOCK, held[mine, :], 0.0))
        pause()

        def below(t, inner):
            rows = pl.ds(pl.multiple_of(t * BLOCK, BLOCK), BLOCK)
            held[rows, mine] = jnp.zeros(shape, jnp.float32)
            held[rows, :] = held[rows, :] - dot(held[mine, rows], held[mine, :], 0, 0, HIGHEST)
            return inner

        lax.fori_loop(k + 1, count, below, 0)
        return carry

    lax.fori_loop(0, count, step, 0)


def factors(momentum, gradient, basis):
    f32, bf16 = jnp.float32, jnp.bfloat16
    rows, columns = momentum.shape
    vmem = pl.BlockSpec(memory_space=pltpu.VMEM)
    return pl.pallas_call(
        main_kernel,
        out_shape=[
            jax.ShapeDtypeStruct((columns, RANK), bf16),
            jax.ShapeDtypeStruct((columns, RANK), bf16),
            jax.ShapeDtypeStruct((rows, RANK), bf16),
            jax.ShapeDtypeStruct((rows, RANK), bf16),
            jax.ShapeDtypeStruct((rows, RANK), bf16),
            jax.ShapeDtypeStruct((SHARD, RANK), f32),
        ],
        in_specs=[pl.BlockSpec(memory_space=pl.ANY)] * 2 + [vmem],
        out_specs=[vmem] * 6,
        scratch_shapes=[
            pltpu.VMEM((2, 64, columns), f32),
            pltpu.VMEM((2, 64, columns), bf16),
            pltpu.SemaphoreType.DMA((2, 2)),
            pltpu.VMEM((rows, RANK), f32),
            pltpu.VMEM((columns, RANK), f32),
            pltpu.VMEM((RANK, RANK), bf16),
            pltpu.VMEM((RANK, RANK), bf16),
            pltpu.VMEM((8, 8, RANK), f32),
            pltpu.VMEM((columns, RANK), f32),
            pltpu.VMEM((rows, columns), bf16),
            pltpu.VMEM((rows, columns), bf16),
            pltpu.VMEM((rows, RANK), f32),
            pltpu.VMEM((2, 256, WIDE), f32),
            pltpu.VMEM((2, 2, 32, WIDE), f32),
            pltpu.VMEM((2, 2, 64, WIDE), f32),
            pltpu.VMEM((rows, RANK), bf16),
            pltpu.VMEM((rows, RANK), bf16),
            pltpu.VMEM((16, HALF, WIDE), f32),
            pltpu.VMEM((16, SHARD, WIDE), f32),
            pltpu.VMEM((4, HALF, WIDE), f32),
            pltpu.VMEM((4, SHARD, WIDE), f32),
            pltpu.VMEM((RANK, RANK), f32),
            pltpu.VMEM((BLOCK, RANK), f32),
            pltpu.VMEM((16, 8, RANK), f32),
            pltpu.SemaphoreType.DMA((260,)),
            pltpu.SemaphoreType.DMA((260,)),
        ],
        compiler_params=pltpu.CompilerParams(
            collective_id=0, has_side_effects=True, vmem_limit_bytes=63 << 20
        ),
        cost_estimate=pl.CostEstimate(flops=60_000_000_000, bytes_accessed=30 << 20, transcendentals=0),
        name="factors",
    )(momentum, gradient, basis)


def output_kernel(momentum_ref, gradient_ref, rh_ref, rl_ref, oh_ref, sh_ref, sl_ref, momentum_out, update_out):
    rh, rl = rh_ref[...], rl_ref[...]
    dims = (((1,), (1,)), ((), ()))
    low = lax.dot_general(oh_ref[...], rh, dims, preferred_element_type=jnp.float32)
    momentum_out[...] = (momentum_ref[...] + gradient_ref[...].astype(jnp.float32)) - low
    update_out[...] = dot3(sh_ref[...], sl_ref[...], rh, rl, 1, 1).astype(jnp.bfloat16)


def outputs(momentum, gradient, rh, rl, oh, sh, sl):
    rows, columns = momentum.shape
    wide = 256
    tile = pl.BlockSpec((rows, wide), lambda i: (0, i))
    right = pl.BlockSpec((wide, RANK), lambda i: (i, 0))
    whole = pl.BlockSpec((rows, RANK), lambda i: (0, 0))
    return pl.pallas_call(
        output_kernel,
        grid=(columns // wide,),
        out_shape=[
            jax.ShapeDtypeStruct((rows, columns), jnp.float32),
            jax.ShapeDtypeStruct((rows, columns), jnp.bfloat16),
        ],
        in_specs=[tile, tile, right, right, whole, whole, whole],
        out_specs=[tile, tile],
        compiler_params=pltpu.CompilerParams(vmem_limit_bytes=63 << 20),
        name="outputs",
    )(momentum, gradient, rh, rl, oh, sh, sl)


def local(gradient, momentum, basis):
    rh, rl, oh, sh, sl, new_basis = factors(momentum, gradient, basis)
    new_momentum, update = outputs(momentum, gradient, rh, rl, oh, sh, sl)
    return (new_momentum, new_basis, update)


def solution(mesh):
    placed = (P("fsdp", "tp"), P("fsdp", "tp"), P(("tp", "fsdp"), None))
    return jax.shard_map(
        local,
        mesh=mesh,
        in_specs=placed,
        out_specs=(P("fsdp", "tp"), P(("tp", "fsdp"), None), P("fsdp", "tp")),
        check_vma=False,
    )
```

```python
import functools

import jax
import jax.numpy as jnp
from jax import lax
from jax.experimental import pallas as pl
from jax.experimental.pallas import tpu as pltpu
from jax.sharding import PartitionSpec as P

M = 8192
N = 14336
RANK = 1024
BLOCK = 128
STRIP = 8
HIGHEST = lax.Precision.HIGHEST
HIGH = lax.Precision.HIGH
MESH = pl.DeviceIdType.MESH
SHARD = 112
HALF = 56
WIDE = 512


def dot(a, b, ca, cb, precision):
    dims = (((ca,), (cb,)), ((), ()))
    return lax.dot_general(a, b, dims, precision=precision, preferred_element_type=jnp.float32)


def recip(d):
    r = lax.rsqrt(d)
    return r * r


def factor(block, pause):
    shape = (STRIP, BLOCK)
    lane = lax.broadcasted_iota(jnp.int32, shape, 1)
    sub = lax.broadcasted_iota(jnp.int32, shape, 0)
    count = BLOCK // STRIP
    strips = [block[STRIP * t : STRIP * (t + 1), :] for t in range(count)]
    out = []
    for s in range(count):
        if s in (4, 8, 12):
            pause()
        first = STRIP * s
        w = strips[s]
        columns = [jnp.broadcast_to(w[:, first + j : first + j + 1], shape) for j in range(STRIP)]
        a = [[jnp.broadcast_to(columns[j][i : i + 1, :], shape) for j in range(i + 1)] for i in range(STRIP)]
        pivots = jnp.ones(shape, jnp.float32)
        for k in range(STRIP):
            here = lane == first + k
            inverse = recip(a[k][k])
            pivots = jnp.where(sub == k, a[k][k], pivots)
            ratio = {i: a[i][k] * inverse for i in range(k + 1, STRIP)}
            for i in range(k + 1, STRIP):
                for j in range(k + 1, i + 1):
                    a[i][j] = a[i][j] - ratio[i] * a[j][k]
            times = jnp.zeros(shape, jnp.float32)
            for i in range(k + 1, STRIP):
                times = jnp.where(sub == i, ratio[i], times)
            w = jnp.where(here & (sub >= k), jnp.where(sub == k, 1.0, 0.0), w)
            w = w - times * jnp.broadcast_to(w[k : k + 1, :], shape)
        r = w * lax.rsqrt(pivots)
        r = jnp.where((lane > first + sub) & (lane < first + STRIP), 0.0, r)
        out.append(jnp.where(lane <= sub + first, r, 0.0))
        inside = (lane >= first) & (lane < first + STRIP)
        turned = jnp.transpose(r)
        rows = [jnp.broadcast_to(r[i : i + 1, :], shape) for i in range(STRIP)]
        for t in range(s + 1, count):
            total = jnp.where(inside, 0.0, strips[t])
            for i in range(STRIP):
                total = total - jnp.broadcast_to(turned[STRIP * t : STRIP * (t + 1), i : i + 1], shape) * rows[i]
            strips[t] = total
    return jnp.concatenate(out, axis=0)


def split(x):
    high = x.astype(jnp.bfloat16)
    return high, (x - high.astype(jnp.float32)).astype(jnp.bfloat16)


def dot3(ah, al, bh, bl, ca, cb):
    def one(a, b):
        dims = (((ca,), (cb,)), ((), ()))
        return lax.dot_general(a, b, dims, preferred_element_type=jnp.float32)

    return one(ah, bh) + (one(ah, bl) + one(al, bh))


class Net:
    def __init__(self, send_sem, recv_sem):
        self.send_sem, self.recv_sem, self.made, self.open = send_sem, recv_sem, {}, []
        self.index, self.dry = {}, False
        fsdp, tp = lax.axis_index("fsdp"), lax.axis_index("tp")
        self.y, self.z = fsdp // 4, fsdp % 4
        self.x, self.core = tp // 2, tp % 2

    def at(self, y=0, z=0, x=0, core=0):
        f = ((self.y + y + 4) % 4) * 4 + (self.z + z + 4) % 4
        t = ((self.x + x + 4) % 4) * 2 + (self.core + core) % 2
        return (f, t)

    def send(self, key, source, target, to):
        i = self.index.setdefault(key, len(self.index))

        def make():
            return pltpu.make_async_remote_copy(
                src_ref=source(),
                dst_ref=target(),
                send_sem=self.send_sem.at[i],
                recv_sem=self.recv_sem.at[i],
                device_id=self.at(**to),
                device_id_type=MESH,
            )

        self.made[key] = make
        if not self.dry:
            self.open.append(key)
            make().start()

    def got(self, *keys):
        for key in () if self.dry else keys:
            self.made[key]().wait_recv()

    def sent(self, name=None):
        done = [key for key in self.open if name is None or key[0] == name]
        for key in done:
            self.made[key]().wait_send()
        self.open = [key for key in self.open if key not in done]


def shard_of(net, ref, first, o1, o2, half, part):
    dy, dz = (o1, o2) if first == "y" else (o2, o1)
    index = ((net.y + dy + 4) % 4) * 4 + (net.z + dz + 4) % 4
    at, rows = {"all": (0, SHARD), "top": (0, HALF), "low": (HALF, HALF)}[part]
    return ref.at[pl.ds(pl.multiple_of(index * SHARD + at, 8), rows), pl.ds(half * WIDE, WIDE)]


def gather_events(net, name, own, buf):
    lists = []
    for half, (d1, d2) in enumerate((("y", "z"), ("z", "y"))):
        key = lambda *k, half=half: (name, half) + k
        shard = lambda o1, o2, part="all", d1=d1, half=half: shard_of(net, buf, d1, o1, o2, half, part)

        def both(o, key=key, shard=shard, d2=d2):
            for way, sign in ((1, "+"), (-1, "-")):
                net.send(key(2, o, sign), lambda: shard(o, 0), lambda: shard(o, 0), {d2: way})

        def start(key=key, shard=shard, d1=d1, d2=d2, half=half):
            mine = lambda: own(half)
            for way, sign in ((1, "+"), (-1, "-")):
                net.send(key(1, sign), mine, lambda: shard(0, 0), {d1: way})
            for way, sign in ((1, "+"), (-1, "-")):
                net.send(key(2, 0, sign), mine, lambda: shard(0, 0), {d2: way})

        def near(o, way, sign, part, key=key, shard=shard, d1=d1, both=both):
            net.got(key(1, sign))
            net.send(key(1, "f" + sign), lambda: shard(o, 0, part), lambda: shard(o, 0, part), {d1: way})
            both(o)

        def far(key=key, both=both):
            net.got(key(1, "f+"), key(1, "f-"))
            both(2)

        def pass_on(o, p, way, sign, part, key=key, shard=shard, d2=d2):
            net.got(key(2, o, sign))
            net.send(key(2, o, "f" + sign), lambda: shard(o, p, part), lambda: shard(o, p, part), {d2: way})

        def last(key=key):
            for o in (0, -1, 1, 2):
                net.got(key(2, o, "f+"), key(2, o, "f-"))

        events = [start, functools.partial(near, -1, 1, "+", "top"), functools.partial(near, 1, -1, "-", "low")]
        for i, o in enumerate((0, -1, 1, 2)):
            if i == 1:
                events.append(far)
            events.append(functools.partial(pass_on, o, -1, 1, "+", "top"))
            events.append(functools.partial(pass_on, o, 1, -1, "-", "low"))
        events.append(last)
        lists.append(events)
    return [e for pair in zip(*lists) for e in pair]


def scatter_events(net, name, buf, ra, rb, rc, rd):
    lists = []
    order = (2, 1, -1, 0)
    for half, (e1, e2) in enumerate((("y", "z"), ("z", "y"))):
        key = lambda *k, half=half: (name, half) + k
        shard = lambda o1, o2, part="all", e1=e1, half=half: shard_of(net, buf, e1, o1, o2, half, part)

        def add(ref, *others):
            if net.dry:
                return
            total = ref[...]
            for other in others:
                total = total + other[...]
            ref[...] = total

        def start(o, key=key, shard=shard, e1=e1, half=half):
            i = (half * 4 + order.index(o)) * 2
            net.send(key(1, o, "f+"), lambda: shard(2, o, "top"), lambda: ra.at[i], {e1: 1})
            net.send(key(1, o, "f-"), lambda: shard(2, o, "low"), lambda: ra.at[i + 1], {e1: -1})

        def near(o, way, sign, part, j, key=key, shard=shard, e1=e1, half=half):
            i = (half * 4 + order.index(o)) * 2 + j
            net.got(key(1, o, "f" + sign))
            add(shard(way, o, part), ra.at[i])
            net.send(key(1, o, sign), lambda: shard(way, o), lambda: rb.at[i], {e1: way})

        def line(o, key=key, shard=shard, half=half):
            i = (half * 4 + order.index(o)) * 2
            net.got(key(1, o, "+"), key(1, o, "-"))
            add(shard(0, o), rb.at[i], rb.at[i + 1])

        def far(key=key, shard=shard, e2=e2, half=half, line=line):
            line(2)
            net.send(key(2, "f+"), lambda: shard(0, 2, "top"), lambda: rc.at[2 * half], {e2: 1})
            net.send(key(2, "f-"), lambda: shard(0, 2, "low"), lambda: rc.at[2 * half + 1], {e2: -1})

        def side(way, sign, part, j, key=key, shard=shard, e2=e2, half=half, line=line):
            line(way)
            net.got(key(2, "f" + sign))
            add(shard(0, way, part), rc.at[2 * half + j])
            net.send(key(2, sign), lambda: shard(0, way), lambda: rd.at[2 * half + j], {e2: way})

        def mine(key=key, shard=shard, half=half, line=line):
            line(0)
            net.got(key(2, "+"), key(2, "-"))
            add(shard(0, 0), rd.at[2 * half], rd.at[2 * half + 1])

        events = [functools.partial(start, o) for o in order]
        for o in order:
            events.append(functools.partial(near, o, 1, "+", "top", 0))
            events.append(functools.partial(near, o, -1, "-", "low", 1))
            if o == 1:
                events.append(far)
        events.append(functools.partial(side, 1, "+", "top", 0))
        events.append(functools.partial(side, -1, "-", "low", 1))
        events.append(mine)
        lists.append(events)
    return [e for pair in zip(*lists) for e in pair]


def tp_gather_events(net, name, ref, piece, start_of):
    def part(dx, which="all"):
        at, rows = {"all": (0, piece), "top": (0, piece // 2), "low": (piece // 2, piece // 2)}[which]
        return ref.at[pl.ds(pl.multiple_of(start_of(dx) + at, 8), rows), :]

    def put(key, dx, which, to):
        net.send((name,) + key, lambda: part(dx, which), lambda: part(dx, which), to)

    def start():
        put(("+",), 0, "all", {"x": 1})
        put(("-",), 0, "all", {"x": -1})
        put(("c", 0), 0, "all", {"core": 1})

    def near():
        net.got((name, "+"))
        put(("f+",), -1, "top", {"x": 1})
        net.got((name, "-"))
        put(("f-",), 1, "low", {"x": -1})
        put(("c", -1), -1, "all", {"core": 1})
        put(("c", 1), 1, "all", {"core": 1})

    def last():
        net.got((name, "f+"), (name, "f-"))
        put(("c", 2), 2, "all", {"core": 1})
        net.got(*[(name, "c", dx) for dx in (0, -1, 1, 2)])

    return start, near, last


def tp_sum(net, ref, out, lc, la, lb):
    mine = net.core * 256
    other = 256 - mine
    net.send(("core",), lambda: ref.at[pl.ds(pl.multiple_of(other, 8), 256), :], lambda: lc, {"core": 1})
    net.got(("core",))
    rows = pl.ds(pl.multiple_of(mine, 8), 256)
    ref[rows, :] = ref[rows, :] + lc[...]

    def start_of(dx):
        return mine + ((net.x + dx + 4) % 4) * 64

    def piece(dx, at=0, count=64):
        return ref.at[pl.ds(pl.multiple_of(start_of(dx) + at, 8), count), :]

    net.send(("xf+",), lambda: piece(2, 0, 32), lambda: la.at[0], {"x": 1})
    net.send(("xf-",), lambda: piece(2, 32, 32), lambda: la.at[1], {"x": -1})
    for way, sign, at, j in ((1, "+", 0, 0), (-1, "-", 32, 1)):
        net.got(("xf" + sign,))
        there = piece(way, at, 32)
        there[...] = there[...] + la[j]
        net.send(("x" + sign,), lambda way=way: piece(way), lambda j=j: lb.at[j], {"x": way})
    net.got(("x+",), ("x-",))
    out[pl.ds(pl.multiple_of(start_of(0), 8), 64), :] = piece(0)[...] + lb[0] + lb[1]
    for event in tp_gather_events(net, "left", out, 64, start_of):
        event()


def main_kernel(
    momentum_ref, gradient_ref, basis_ref, rh, rl, oh, sh, sl, basis_out,
    momentum_in, gradient_in, in_sem, left_ref, cross_ref, ih, il, sq, buf, mh, ml, lbuf, lc, la, lb, lh, ll, ra, rb, rc, rd, held, gpart, gsum, send_sem, recv_sem,
):
    net = Net(send_sem, recv_sem)
    me = net.y * 4 + net.z
    tp = net.x * 2 + net.core
    barrier = pltpu.get_barrier_semaphore()
    for i in range(1, 16):
        pl.semaphore_signal(barrier, inc=1, device_id=((me + i) % 16, tp), device_id_type=MESH)
    for i in range(1, 8):
        pl.semaphore_signal(barrier, inc=1, device_id=(me, (tp + i) % 8), device_id_type=MESH)
    pl.semaphore_wait(barrier, 15 + 7)

    events = gather_events(net, "basis", lambda half: basis_ref.at[:, pl.ds(half * WIDE, WIDE)], buf)
    for event in events[:2]:
        event()
    buf[pl.ds(pl.multiple_of(me * SHARD, 8), SHARD), :] = basis_ref[...]

    def load(i, slot):
        rows = pl.ds(pl.multiple_of(i * 64, 64), 64)
        return (
            pltpu.make_async_copy(momentum_ref.at[rows, :], momentum_in.at[slot], in_sem.at[0, slot]),
            pltpu.make_async_copy(gradient_ref.at[rows, :], gradient_in.at[slot], in_sem.at[1, slot]),
        )

    for i in range(8):
        if i == 0:
            for copy in load(0, 0):
                copy.start()
        if i < 7:
            for copy in load(i + 1, (i + 1) % 2):
                copy.start()
        for copy in load(i, i % 2):
            copy.wait()
        rows = slice(64 * i, 64 * i + 64)
        mh[rows, :], ml[rows, :] = split(momentum_in[i % 2] + gradient_in[i % 2].astype(jnp.float32))

    for event in events[2:]:
        event()

    @pl.loop(0, 4)
    def _(i):
        columns = pl.ds(pl.multiple_of(i * 256, 256), 256)
        bh, bl = split(buf[:, columns])
        lbuf[:, columns] = dot3(mh[...], ml[...], bh, bl, 1, 0)

    tp_sum(net, lbuf, left_ref, lc, la, lb)
    net.sent()

    own_rows = pl.ds(pl.multiple_of(tp * BLOCK, BLOCK), BLOCK)
    gpart[...] = dot(left_ref[:, own_rows], left_ref[...], 0, 0, HIGHEST)
    copies = []
    for i in range(1, 16):
        to = (me + i) % 16
        copies.append(
            pltpu.make_async_remote_copy(
                src_ref=gpart.at[pl.ds(pl.multiple_of(to * 8, 8), 8), :],
                dst_ref=gsum.at[i],
                send_sem=send_sem.at[150 + i],
                recv_sem=recv_sem.at[150 + i],
                device_id=(to, tp),
                device_id_type=MESH,
            )
        )
        copies[-1].start()

    lh[...], ll[...] = split(left_ref[...])

    @pl.loop(0, 7)
    def _(i):
        columns = pl.ds(pl.multiple_of(i * 256, 256), 256)
        buf[columns, :] = dot3(mh[:, columns], ml[:, columns], lh[...], ll[...], 0, 0)

    scatter = scatter_events(net, "scatter", buf, ra, rb, rc, rd)
    for copy in copies:
        copy.wait()
    total = gpart[pl.ds(pl.multiple_of(me * 8, 8), 8), :]
    for i in range(1, 16):
        total = total + gsum[i]
    at = pl.multiple_of(tp * BLOCK + me * 8, 8)
    held[pl.ds(at, 8), :] = total
    copies = []
    for i in range(1, 16):
        copies.append(
            pltpu.make_async_remote_copy(
                src_ref=held.at[pl.ds(at, 8), :],
                dst_ref=held.at[pl.ds(at, 8), :],
                send_sem=send_sem.at[170 + i],
                recv_sem=recv_sem.at[170 + i],
                device_id=((me + i) % 16, tp),
                device_id_type=MESH,
            )
        )
        copies[-1].start()
    for event in scatter[:12]:
        event()
    for copy in copies:
        copy.wait()
    gram_events = tp_gather_events(
        net, "gram", held, BLOCK, lambda dx: (((net.x + dx + 4) % 4) * 2 + net.core) * BLOCK
    )
    gram_events[0]()
    for event in scatter[12:18]:
        event()
    gram_events[1]()
    for event in scatter[18:22]:
        event()
    gram_events[2]()
    net.sent("gram")

    def own(half):
        return shard_of(net, buf, "y", 0, 0, half, "all")

    def keep():
        if net.dry:
            return
        rows = pl.ds(pl.multiple_of(me * SHARD, 8), SHARD)
        cross_ref[rows, :] = buf[rows, :]

    rest = scatter[22:] + [keep] + gather_events(net, "cross", own, cross_ref)
    eliminate(net, held, ih, il, rest)
    net.sent()

    sq[0] = jnp.zeros((8, RANK), jnp.float32)

    @pl.loop(0, 7)
    def _(i):
        rows = pl.ds(pl.multiple_of(i * 256, 256), 256)
        wh, wl = split(cross_ref[rows, :])
        for n in range(4):
            upto = 256 * (n + 1)
            block = slice(256 * n, upto)
            part = dot3(wh[:, :upto], wl[:, :upto], ih[block, :upto], il[block, :upto], 1, 1)
            rh[rows, block], rl[rows, block] = split(part)
            sq[0, :, block] = sq[0, :, block] + jnp.sum((part * part).reshape(32, 8, 256), axis=0)

    copies = []
    for i in range(1, 8):
        copies.append(
            pltpu.make_async_remote_copy(
                src_ref=sq.at[0],
                dst_ref=sq.at[i],
                send_sem=send_sem.at[190 + i],
                recv_sem=recv_sem.at[190 + i],
                device_id=(me, (tp + i) % 8),
                device_id_type=MESH,
            )
        )
        copies[-1].start()
    for n in range(4):
        upto = 256 * (n + 1)
        block = slice(256 * n, upto)
        lbuf[:, block] = dot3(lh[:, :upto], ll[:, :upto], ih[block, :upto], il[block, :upto], 1, 1)
    oh[...] = (0.05 * lbuf[...]).astype(jnp.bfloat16)
    for copy in copies:
        copy.wait()
    total = sq[0]
    for i in range(1, 8):
        total = total + sq[i]
    over = 1.0 / jnp.sqrt(jnp.sum(total, axis=0, keepdims=True) + 1e-08)
    scale = jnp.sqrt(jnp.float32(M) * jnp.float32(N) / jnp.float32(RANK))
    sh[...], sl[...] = split(lbuf[...] * (scale * over))
    rows = pl.ds(pl.multiple_of(me * SHARD, 16), SHARD)
    basis_out[...] = (rh[rows, :].astype(jnp.float32) + rl[rows, :].astype(jnp.float32)) * over


def eliminate(net, held, ih, il, events):
    n = held.shape[0]
    count = n // BLOCK
    shape = (BLOCK, BLOCK)
    eye = (lax.broadcasted_iota(jnp.int32, shape, 0) == lax.broadcasted_iota(jnp.int32, shape, 1)).astype(jnp.float32)
    lanes = lax.broadcasted_iota(jnp.int32, (BLOCK, n), 1)
    slots = 5 * count
    plan = [events[len(events) * i // slots : len(events) * (i + 1) // slots] for i in range(slots)]
    net.dry = True
    for event in events:
        event()
    net.dry = False

    def step(k, carry):
        used = []

        def pause():
            for i in range(count):
                group = plan[5 * i + len(used)]
                if group:

                    @pl.when(k == i)
                    def _():
                        for event in group:
                            event()

            used.append(None)

        mine = pl.ds(pl.multiple_of(k * BLOCK, BLOCK), BLOCK)
        pause()
        inverse = factor(held[mine, mine], pause)
        held[mine, mine] = eye
        held[mine, :] = dot(inverse, held[mine, :], 1, 0, HIGHEST)
        ih[mine, :], il[mine, :] = split(jnp.where(lanes < (k + 1) * BLOCK, held[mine, :], 0.0))
        pause()

        def below(t, inner):
            rows = pl.ds(pl.multiple_of(t * BLOCK, BLOCK), BLOCK)
            held[rows, mine] = jnp.zeros(shape, jnp.float32)
            held[rows, :] = held[rows, :] - dot(held[mine, rows], held[mine, :], 0, 0, HIGHEST)
            return inner

        lax.fori_loop(k + 1, count, below, 0)
        return carry

    lax.fori_loop(0, count, step, 0)


def factors(momentum, gradient, basis):
    f32, bf16 = jnp.float32, jnp.bfloat16
    rows, columns = momentum.shape
    vmem = pl.BlockSpec(memory_space=pltpu.VMEM)
    return pl.pallas_call(
        main_kernel,
        out_shape=[
            jax.ShapeDtypeStruct((columns, RANK), bf16),
            jax.ShapeDtypeStruct((columns, RANK), bf16),
            jax.ShapeDtypeStruct((rows, RANK), bf16),
            jax.ShapeDtypeStruct((rows, RANK), bf16),
            jax.ShapeDtypeStruct((rows, RANK), bf16),
            jax.ShapeDtypeStruct((SHARD, RANK), f32),
        ],
        in_specs=[pl.BlockSpec(memory_space=pl.ANY)] * 2 + [vmem],
        out_specs=[vmem] * 6,
        scratch_shapes=[
            pltpu.VMEM((2, 64, columns), f32),
            pltpu.VMEM((2, 64, columns), bf16),
            pltpu.SemaphoreType.DMA((2, 2)),
            pltpu.VMEM((rows, RANK), f32),
            pltpu.VMEM((columns, RANK), f32),
            pltpu.VMEM((RANK, RANK), bf16),
            pltpu.VMEM((RANK, RANK), bf16),
            pltpu.VMEM((8, 8, RANK), f32),
            pltpu.VMEM((columns, RANK), f32),
            pltpu.VMEM((rows, columns), bf16),
            pltpu.VMEM((rows, columns), bf16),
            pltpu.VMEM((rows, RANK), f32),
            pltpu.VMEM((256, RANK), f32),
            pltpu.VMEM((2, 32, RANK), f32),
            pltpu.VMEM((2, 64, RANK), f32),
            pltpu.VMEM((rows, RANK), bf16),
            pltpu.VMEM((rows, RANK), bf16),
            pltpu.VMEM((16, HALF, WIDE), f32),
            pltpu.VMEM((16, SHARD, WIDE), f32),
            pltpu.VMEM((4, HALF, WIDE), f32),
            pltpu.VMEM((4, SHARD, WIDE), f32),
            pltpu.VMEM((RANK, RANK), f32),
            pltpu.VMEM((BLOCK, RANK), f32),
            pltpu.VMEM((16, 8, RANK), f32),
            pltpu.SemaphoreType.DMA((200,)),
            pltpu.SemaphoreType.DMA((200,)),
        ],
        compiler_params=pltpu.CompilerParams(
            collective_id=0, has_side_effects=True, vmem_limit_bytes=63 << 20
        ),
        cost_estimate=pl.CostEstimate(flops=60_000_000_000, bytes_accessed=30 << 20, transcendentals=0),
        name="factors",
    )(momentum, gradient, basis)


def output_kernel(momentum_ref, gradient_ref, rh_ref, rl_ref, oh_ref, sh_ref, sl_ref, momentum_out, update_out):
    rh, rl = rh_ref[...], rl_ref[...]
    dims = (((1,), (1,)), ((), ()))
    low = lax.dot_general(oh_ref[...], rh, dims, preferred_element_type=jnp.float32)
    momentum_out[...] = (momentum_ref[...] + gradient_ref[...].astype(jnp.float32)) - low
    update_out[...] = dot3(sh_ref[...], sl_ref[...], rh, rl, 1, 1).astype(jnp.bfloat16)


def outputs(momentum, gradient, rh, rl, oh, sh, sl):
    rows, columns = momentum.shape
    wide = 256
    tile = pl.BlockSpec((rows, wide), lambda i: (0, i))
    right = pl.BlockSpec((wide, RANK), lambda i: (i, 0))
    whole = pl.BlockSpec((rows, RANK), lambda i: (0, 0))
    return pl.pallas_call(
        output_kernel,
        grid=(columns // wide,),
        out_shape=[
            jax.ShapeDtypeStruct((rows, columns), jnp.float32),
            jax.ShapeDtypeStruct((rows, columns), jnp.bfloat16),
        ],
        in_specs=[tile, tile, right, right, whole, whole, whole],
        out_specs=[tile, tile],
        compiler_params=pltpu.CompilerParams(vmem_limit_bytes=63 << 20),
        name="outputs",
    )(momentum, gradient, rh, rl, oh, sh, sl)


def local(gradient, momentum, basis):
    rh, rl, oh, sh, sl, new_basis = factors(momentum, gradient, basis)
    new_momentum, update = outputs(momentum, gradient, rh, rl, oh, sh, sl)
    return (new_momentum, new_basis, update)


def solution(mesh):
    placed = (P("fsdp", "tp"), P("fsdp", "tp"), P(("tp", "fsdp"), None))
    return jax.shard_map(
        local,
        mesh=mesh,
        in_specs=placed,
        out_specs=(P("fsdp", "tp"), P(("tp", "fsdp"), None), P("fsdp", "tp")),
        check_vma=False,
    )
```

```python
import functools

import jax
import jax.numpy as jnp
from jax import lax
from jax.experimental import pallas as pl
from jax.experimental.pallas import tpu as pltpu
from jax.sharding import PartitionSpec as P

M = 8192
N = 14336
RANK = 1024
BLOCK = 128
STRIP = 8
HIGHEST = lax.Precision.HIGHEST
HIGH = lax.Precision.HIGH
MESH = pl.DeviceIdType.MESH
SHARD = 112
HALF = 56
WIDE = 512


def dot(a, b, ca, cb, precision):
    dims = (((ca,), (cb,)), ((), ()))
    return lax.dot_general(a, b, dims, precision=precision, preferred_element_type=jnp.float32)


def recip(d):
    r = lax.rsqrt(d)
    return r * r


def factor(block, pause):
    shape = (STRIP, BLOCK)
    lane = lax.broadcasted_iota(jnp.int32, shape, 1)
    sub = lax.broadcasted_iota(jnp.int32, shape, 0)
    count = BLOCK // STRIP
    strips = [block[STRIP * t : STRIP * (t + 1), :] for t in range(count)]
    out = []
    for s in range(count):
        if s in (4, 8, 12):
            pause()
        first = STRIP * s
        w = strips[s]
        columns = [jnp.broadcast_to(w[:, first + j : first + j + 1], shape) for j in range(STRIP)]
        a = [[jnp.broadcast_to(columns[j][i : i + 1, :], shape) for j in range(i + 1)] for i in range(STRIP)]
        pivots = jnp.ones(shape, jnp.float32)
        for k in range(STRIP):
            here = lane == first + k
            inverse = recip(a[k][k])
            pivots = jnp.where(sub == k, a[k][k], pivots)
            ratio = {i: a[i][k] * inverse for i in range(k + 1, STRIP)}
            for i in range(k + 1, STRIP):
                for j in range(k + 1, i + 1):
                    a[i][j] = a[i][j] - ratio[i] * a[j][k]
            times = jnp.zeros(shape, jnp.float32)
            for i in range(k + 1, STRIP):
                times = jnp.where(sub == i, ratio[i], times)
            w = jnp.where(here & (sub >= k), jnp.where(sub == k, 1.0, 0.0), w)
            w = w - times * jnp.broadcast_to(w[k : k + 1, :], shape)
        r = w * lax.rsqrt(pivots)
        r = jnp.where((lane > first + sub) & (lane < first + STRIP), 0.0, r)
        out.append(jnp.where(lane <= sub + first, r, 0.0))
        inside = (lane >= first) & (lane < first + STRIP)
        turned = jnp.transpose(r)
        rows = [jnp.broadcast_to(r[i : i + 1, :], shape) for i in range(STRIP)]
        for t in range(s + 1, count):
            total = jnp.where(inside, 0.0, strips[t])
            for i in range(STRIP):
                total = total - jnp.broadcast_to(turned[STRIP * t : STRIP * (t + 1), i : i + 1], shape) * rows[i]
            strips[t] = total
    return jnp.concatenate(out, axis=0)


def split(x):
    high = x.astype(jnp.bfloat16)
    return high, (x - high.astype(jnp.float32)).astype(jnp.bfloat16)


def dot3(ah, al, bh, bl, ca, cb):
    def one(a, b):
        dims = (((ca,), (cb,)), ((), ()))
        return lax.dot_general(a, b, dims, preferred_element_type=jnp.float32)

    return one(ah, bh) + (one(ah, bl) + one(al, bh))


class Net:
    def __init__(self, send_sem, recv_sem):
        self.send_sem, self.recv_sem, self.made, self.open = send_sem, recv_sem, {}, []
        self.index, self.dry = {}, False
        fsdp, tp = lax.axis_index("fsdp"), lax.axis_index("tp")
        self.y, self.z = fsdp // 4, fsdp % 4
        self.x, self.core = tp // 2, tp % 2

    def at(self, y=0, z=0, x=0, core=0):
        f = ((self.y + y + 4) % 4) * 4 + (self.z + z + 4) % 4
        t = ((self.x + x + 4) % 4) * 2 + (self.core + core) % 2
        return (f, t)

    def send(self, key, source, target, to):
        i = self.index.setdefault(key, len(self.index))

        def make():
            return pltpu.make_async_remote_copy(
                src_ref=source(),
                dst_ref=target(),
                send_sem=self.send_sem.at[i],
                recv_sem=self.recv_sem.at[i],
                device_id=self.at(**to),
                device_id_type=MESH,
            )

        self.made[key] = make
        if not self.dry:
            self.open.append(key)
            make().start()

    def got(self, *keys):
        for key in () if self.dry else keys:
            self.made[key]().wait_recv()

    def sent(self, name=None):
        done = [key for key in self.open if name is None or key[0] == name]
        for key in done:
            self.made[key]().wait_send()
        self.open = [key for key in self.open if key not in done]


def shard_of(net, ref, first, o1, o2, half, part):
    dy, dz = (o1, o2) if first == "y" else (o2, o1)
    index = ((net.y + dy + 4) % 4) * 4 + (net.z + dz + 4) % 4
    at, rows = {"all": (0, SHARD), "top": (0, HALF), "low": (HALF, HALF)}[part]
    return ref.at[pl.ds(pl.multiple_of(index * SHARD + at, 8), rows), pl.ds(half * WIDE, WIDE)]


def gather_events(net, name, own, buf):
    lists = []
    for half, (d1, d2) in enumerate((("y", "z"), ("z", "y"))):
        key = lambda *k, half=half: (name, half) + k
        shard = lambda o1, o2, part="all", d1=d1, half=half: shard_of(net, buf, d1, o1, o2, half, part)

        def both(o, key=key, shard=shard, d2=d2):
            for way, sign in ((1, "+"), (-1, "-")):
                net.send(key(2, o, sign), lambda: shard(o, 0), lambda: shard(o, 0), {d2: way})

        def start(key=key, shard=shard, d1=d1, d2=d2, half=half):
            mine = lambda: own(half)
            for way, sign in ((1, "+"), (-1, "-")):
                net.send(key(1, sign), mine, lambda: shard(0, 0), {d1: way})
            for way, sign in ((1, "+"), (-1, "-")):
                net.send(key(2, 0, sign), mine, lambda: shard(0, 0), {d2: way})

        def near(o, way, sign, part, key=key, shard=shard, d1=d1, both=both):
            net.got(key(1, sign))
            net.send(key(1, "f" + sign), lambda: shard(o, 0, part), lambda: shard(o, 0, part), {d1: way})
            both(o)

        def far(key=key, both=both):
            net.got(key(1, "f+"), key(1, "f-"))
            both(2)

        def pass_on(o, p, way, sign, part, key=key, shard=shard, d2=d2):
            net.got(key(2, o, sign))
            net.send(key(2, o, "f" + sign), lambda: shard(o, p, part), lambda: shard(o, p, part), {d2: way})

        def last(key=key):
            for o in (0, -1, 1, 2):
                net.got(key(2, o, "f+"), key(2, o, "f-"))

        events = [start, functools.partial(near, -1, 1, "+", "top"), functools.partial(near, 1, -1, "-", "low")]
        for i, o in enumerate((0, -1, 1, 2)):
            if i == 1:
                events.append(far)
            events.append(functools.partial(pass_on, o, -1, 1, "+", "top"))
            events.append(functools.partial(pass_on, o, 1, -1, "-", "low"))
        events.append(last)
        lists.append(events)
    return [e for pair in zip(*lists) for e in pair]


def scatter_events(net, name, buf, ra, rb, rc, rd):
    lists = []
    order = (2, 1, -1, 0)
    for half, (e1, e2) in enumerate((("y", "z"), ("z", "y"))):
        key = lambda *k, half=half: (name, half) + k
        shard = lambda o1, o2, part="all", e1=e1, half=half: shard_of(net, buf, e1, o1, o2, half, part)

        def add(ref, *others):
            if net.dry:
                return
            total = ref[...]
            for other in others:
                total = total + other[...]
            ref[...] = total

        def start(o, key=key, shard=shard, e1=e1, half=half):
            i = (half * 4 + order.index(o)) * 2
            net.send(key(1, o, "f+"), lambda: shard(2, o, "top"), lambda: ra.at[i], {e1: 1})
            net.send(key(1, o, "f-"), lambda: shard(2, o, "low"), lambda: ra.at[i + 1], {e1: -1})

        def near(o, way, sign, part, j, key=key, shard=shard, e1=e1, half=half):
            i = (half * 4 + order.index(o)) * 2 + j
            net.got(key(1, o, "f" + sign))
            add(shard(way, o, part), ra.at[i])
            net.send(key(1, o, sign), lambda: shard(way, o), lambda: rb.at[i], {e1: way})

        def line(o, key=key, shard=shard, half=half):
            i = (half * 4 + order.index(o)) * 2
            net.got(key(1, o, "+"), key(1, o, "-"))
            add(shard(0, o), rb.at[i], rb.at[i + 1])

        def far(key=key, shard=shard, e2=e2, half=half, line=line):
            line(2)
            net.send(key(2, "f+"), lambda: shard(0, 2, "top"), lambda: rc.at[2 * half], {e2: 1})
            net.send(key(2, "f-"), lambda: shard(0, 2, "low"), lambda: rc.at[2 * half + 1], {e2: -1})

        def side(way, sign, part, j, key=key, shard=shard, e2=e2, half=half, line=line):
            line(way)
            net.got(key(2, "f" + sign))
            add(shard(0, way, part), rc.at[2 * half + j])
            net.send(key(2, sign), lambda: shard(0, way), lambda: rd.at[2 * half + j], {e2: way})

        def mine(key=key, shard=shard, half=half, line=line):
            line(0)
            net.got(key(2, "+"), key(2, "-"))
            add(shard(0, 0), rd.at[2 * half], rd.at[2 * half + 1])

        events = [functools.partial(start, o) for o in order]
        for o in order:
            events.append(functools.partial(near, o, 1, "+", "top", 0))
            events.append(functools.partial(near, o, -1, "-", "low", 1))
            if o == 1:
                events.append(far)
        events.append(functools.partial(side, 1, "+", "top", 0))
        events.append(functools.partial(side, -1, "-", "low", 1))
        events.append(mine)
        lists.append(events)
    return [e for pair in zip(*lists) for e in pair]


def tp_gather_events(net, name, ref, piece, start_of):
    def part(dx, which="all"):
        at, rows = {"all": (0, piece), "top": (0, piece // 2), "low": (piece // 2, piece // 2)}[which]
        return ref.at[pl.ds(pl.multiple_of(start_of(dx) + at, 8), rows), :]

    def put(key, dx, which, to):
        net.send((name,) + key, lambda: part(dx, which), lambda: part(dx, which), to)

    def start():
        put(("+",), 0, "all", {"x": 1})
        put(("-",), 0, "all", {"x": -1})
        put(("c", 0), 0, "all", {"core": 1})

    def near():
        net.got((name, "+"))
        put(("f+",), -1, "top", {"x": 1})
        net.got((name, "-"))
        put(("f-",), 1, "low", {"x": -1})
        put(("c", -1), -1, "all", {"core": 1})
        put(("c", 1), 1, "all", {"core": 1})

    def last():
        net.got((name, "f+"), (name, "f-"))
        put(("c", 2), 2, "all", {"core": 1})
        net.got(*[(name, "c", dx) for dx in (0, -1, 1, 2)])

    return start, near, last


def tp_sum(net, ref, out, lc, la, lb):
    mine = net.core * 256
    other = 256 - mine
    net.send(("core",), lambda: ref.at[pl.ds(pl.multiple_of(other, 8), 256), :], lambda: lc, {"core": 1})
    net.got(("core",))
    rows = pl.ds(pl.multiple_of(mine, 8), 256)
    ref[rows, :] = ref[rows, :] + lc[...]

    def start_of(dx):
        return mine + ((net.x + dx + 4) % 4) * 64

    def piece(dx, at=0, count=64):
        return ref.at[pl.ds(pl.multiple_of(start_of(dx) + at, 8), count), :]

    net.send(("xf+",), lambda: piece(2, 0, 32), lambda: la.at[0], {"x": 1})
    net.send(("xf-",), lambda: piece(2, 32, 32), lambda: la.at[1], {"x": -1})
    for way, sign, at, j in ((1, "+", 0, 0), (-1, "-", 32, 1)):
        net.got(("xf" + sign,))
        there = piece(way, at, 32)
        there[...] = there[...] + la[j]
        net.send(("x" + sign,), lambda way=way: piece(way), lambda j=j: lb.at[j], {"x": way})
    net.got(("x+",), ("x-",))
    out[pl.ds(pl.multiple_of(start_of(0), 8), 64), :] = piece(0)[...] + lb[0] + lb[1]
    for event in tp_gather_events(net, "left", out, 64, start_of):
        event()


def main_kernel(
    momentum_ref, gradient_ref, basis_ref, rh, rl, oh, sh, sl, basis_out,
    momentum_in, gradient_in, in_sem, left_ref, cross_ref, ih, il, sq, buf, mh, ml, lbuf, lc, la, lb, lh, ll, ra, rb, rc, rd, held, gpart, gsum, send_sem, recv_sem,
):
    net = Net(send_sem, recv_sem)
    me = net.y * 4 + net.z
    tp = net.x * 2 + net.core
    barrier = pltpu.get_barrier_semaphore()
    for i in range(1, 16):
        pl.semaphore_signal(barrier, inc=1, device_id=((me + i) % 16, tp), device_id_type=MESH)
    for i in range(1, 8):
        pl.semaphore_signal(barrier, inc=1, device_id=(me, (tp + i) % 8), device_id_type=MESH)
    pl.semaphore_wait(barrier, 15 + 7)

    events = gather_events(net, "basis", lambda half: basis_ref.at[:, pl.ds(half * WIDE, WIDE)], buf)
    for event in events[:2]:
        event()
    buf[pl.ds(pl.multiple_of(me * SHARD, 8), SHARD), :] = basis_ref[...]

    def load(i, slot):
        rows = pl.ds(pl.multiple_of(i * 64, 64), 64)
        return (
            pltpu.make_async_copy(momentum_ref.at[rows, :], momentum_in.at[slot], in_sem.at[0, slot]),
            pltpu.make_async_copy(gradient_ref.at[rows, :], gradient_in.at[slot], in_sem.at[1, slot]),
        )

    for i in range(8):
        if i == 0:
            for copy in load(0, 0):
                copy.start()
        if i < 7:
            for copy in load(i + 1, (i + 1) % 2):
                copy.start()
        for copy in load(i, i % 2):
            copy.wait()
        rows = slice(64 * i, 64 * i + 64)
        mh[rows, :], ml[rows, :] = split(momentum_in[i % 2] + gradient_in[i % 2].astype(jnp.float32))

    for event in events[2:]:
        event()

    @pl.loop(0, 4)
    def _(i):
        columns = pl.ds(pl.multiple_of(i * 256, 256), 256)
        bh, bl = split(buf[:, columns])
        lbuf[:, columns] = dot3(mh[...], ml[...], bh, bl, 1, 0)

    tp_sum(net, lbuf, left_ref, lc, la, lb)
    net.sent()

    own_rows = pl.ds(pl.multiple_of(tp * BLOCK, BLOCK), BLOCK)
    gpart[...] = dot(left_ref[:, own_rows], left_ref[...], 0, 0, HIGHEST)
    copies = []
    for i in range(1, 16):
        to = (me + i) % 16
        copies.append(
            pltpu.make_async_remote_copy(
                src_ref=gpart.at[pl.ds(pl.multiple_of(to * 8, 8), 8), :],
                dst_ref=gsum.at[i],
                send_sem=send_sem.at[150 + i],
                recv_sem=recv_sem.at[150 + i],
                device_id=(to, tp),
                device_id_type=MESH,
            )
        )
        copies[-1].start()

    lh[...], ll[...] = split(left_ref[...])

    @pl.loop(0, 7)
    def _(i):
        columns = pl.ds(pl.multiple_of(i * 256, 256), 256)
        buf[columns, :] = dot3(mh[:, columns], ml[:, columns], lh[...], ll[...], 0, 0)

    scatter = scatter_events(net, "scatter", buf, ra, rb, rc, rd)
    for copy in copies:
        copy.wait()
    total = gpart[pl.ds(pl.multiple_of(me * 8, 8), 8), :]
    for i in range(1, 16):
        total = total + gsum[i]
    at = pl.multiple_of(tp * BLOCK + me * 8, 8)
    held[pl.ds(at, 8), :] = total
    copies = []
    for i in range(1, 16):
        copies.append(
            pltpu.make_async_remote_copy(
                src_ref=held.at[pl.ds(at, 8), :],
                dst_ref=held.at[pl.ds(at, 8), :],
                send_sem=send_sem.at[170 + i],
                recv_sem=recv_sem.at[170 + i],
                device_id=((me + i) % 16, tp),
                device_id_type=MESH,
            )
        )
        copies[-1].start()
    for event in scatter[:8]:
        event()
    for copy in copies:
        copy.wait()
    gram_events = tp_gather_events(
        net, "gram", held, BLOCK, lambda dx: (((net.x + dx + 4) % 4) * 2 + net.core) * BLOCK
    )
    gram_events[0]()
    for event in scatter[8:14]:
        event()
    gram_events[1]()
    for event in scatter[14:20]:
        event()
    gram_events[2]()
    net.sent("gram")

    def own(half):
        return shard_of(net, buf, "y", 0, 0, half, "all")

    def keep():
        if net.dry:
            return
        rows = pl.ds(pl.multiple_of(me * SHARD, 8), SHARD)
        cross_ref[rows, :] = buf[rows, :]

    rest = scatter[20:] + [keep] + gather_events(net, "cross", own, cross_ref)
    eliminate(net, held, ih, il, rest)
    net.sent()

    sq[0] = jnp.zeros((8, RANK), jnp.float32)

    @pl.loop(0, 7)
    def _(i):
        rows = pl.ds(pl.multiple_of(i * 256, 256), 256)
        wh, wl = split(cross_ref[rows, :])
        for n in range(4):
            upto = 256 * (n + 1)
            block = slice(256 * n, upto)
            part = dot3(wh[:, :upto], wl[:, :upto], ih[block, :upto], il[block, :upto], 1, 1)
            rh[rows, block], rl[rows, block] = split(part)
            sq[0, :, block] = sq[0, :, block] + jnp.sum((part * part).reshape(32, 8, 256), axis=0)

    copies = []
    for i in range(1, 8):
        copies.append(
            pltpu.make_async_remote_copy(
                src_ref=sq.at[0],
                dst_ref=sq.at[i],
                send_sem=send_sem.at[190 + i],
                recv_sem=recv_sem.at[190 + i],
                device_id=(me, (tp + i) % 8),
                device_id_type=MESH,
            )
        )
        copies[-1].start()
    for n in range(4):
        upto = 256 * (n + 1)
        block = slice(256 * n, upto)
        lbuf[:, block] = dot3(lh[:, :upto], ll[:, :upto], ih[block, :upto], il[block, :upto], 1, 1)
    oh[...] = (0.05 * lbuf[...]).astype(jnp.bfloat16)
    for copy in copies:
        copy.wait()
    total = sq[0]
    for i in range(1, 8):
        total = total + sq[i]
    over = 1.0 / jnp.sqrt(jnp.sum(total, axis=0, keepdims=True) + 1e-08)
    scale = jnp.sqrt(jnp.float32(M) * jnp.float32(N) / jnp.float32(RANK))
    sh[...], sl[...] = split(lbuf[...] * (scale * over))
    rows = pl.ds(pl.multiple_of(me * SHARD, 16), SHARD)
    basis_out[...] = (rh[rows, :].astype(jnp.float32) + rl[rows, :].astype(jnp.float32)) * over


def eliminate(net, held, ih, il, events):
    n = held.shape[0]
    count = n // BLOCK
    shape = (BLOCK, BLOCK)
    eye = (lax.broadcasted_iota(jnp.int32, shape, 0) == lax.broadcasted_iota(jnp.int32, shape, 1)).astype(jnp.float32)
    lanes = lax.broadcasted_iota(jnp.int32, (BLOCK, n), 1)
    slots = 5 * count
    plan = [events[len(events) * i // slots : len(events) * (i + 1) // slots] for i in range(slots)]
    net.dry = True
    for event in events:
        event()
    net.dry = False

    def step(k, carry):
        used = []

        def pause():
            for i in range(count):
                group = plan[5 * i + len(used)]
                if group:

                    @pl.when(k == i)
                    def _():
                        for event in group:
                            event()

            used.append(None)

        mine = pl.ds(pl.multiple_of(k * BLOCK, BLOCK), BLOCK)
        pause()
        inverse = factor(held[mine, mine], pause)
        held[mine, mine] = eye
        held[mine, :] = dot(inverse, held[mine, :], 1, 0, HIGHEST)
        ih[mine, :], il[mine, :] = split(jnp.where(lanes < (k + 1) * BLOCK, held[mine, :], 0.0))
        pause()

        def below(t, inner):
            rows = pl.ds(pl.multiple_of(t * BLOCK, BLOCK), BLOCK)
            held[rows, mine] = jnp.zeros(shape, jnp.float32)
            held[rows, :] = held[rows, :] - dot(held[mine, rows], held[mine, :], 0, 0, HIGHEST)
            return inner

        lax.fori_loop(k + 1, count, below, 0)
        return carry

    lax.fori_loop(0, count, step, 0)


def factors(momentum, gradient, basis):
    f32, bf16 = jnp.float32, jnp.bfloat16
    rows, columns = momentum.shape
    vmem = pl.BlockSpec(memory_space=pltpu.VMEM)
    return pl.pallas_call(
        main_kernel,
        out_shape=[
            jax.ShapeDtypeStruct((columns, RANK), bf16),
            jax.ShapeDtypeStruct((columns, RANK), bf16),
            jax.ShapeDtypeStruct((rows, RANK), bf16),
            jax.ShapeDtypeStruct((rows, RANK), bf16),
            jax.ShapeDtypeStruct((rows, RANK), bf16),
            jax.ShapeDtypeStruct((SHARD, RANK), f32),
        ],
        in_specs=[pl.BlockSpec(memory_space=pl.ANY)] * 2 + [vmem],
        out_specs=[vmem] * 6,
        scratch_shapes=[
            pltpu.VMEM((2, 64, columns), f32),
            pltpu.VMEM((2, 64, columns), bf16),
            pltpu.SemaphoreType.DMA((2, 2)),
            pltpu.VMEM((rows, RANK), f32),
            pltpu.VMEM((columns, RANK), f32),
            pltpu.VMEM((RANK, RANK), bf16),
            pltpu.VMEM((RANK, RANK), bf16),
            pltpu.VMEM((8, 8, RANK), f32),
            pltpu.VMEM((columns, RANK), f32),
            pltpu.VMEM((rows, columns), bf16),
            pltpu.VMEM((rows, columns), bf16),
            pltpu.VMEM((rows, RANK), f32),
            pltpu.VMEM((256, RANK), f32),
            pltpu.VMEM((2, 32, RANK), f32),
            pltpu.VMEM((2, 64, RANK), f32),
            pltpu.VMEM((rows, RANK), bf16),
            pltpu.VMEM((rows, RANK), bf16),
            pltpu.VMEM((16, HALF, WIDE), f32),
            pltpu.VMEM((16, SHARD, WIDE), f32),
            pltpu.VMEM((4, HALF, WIDE), f32),
            pltpu.VMEM((4, SHARD, WIDE), f32),
            pltpu.VMEM((RANK, RANK), f32),
            pltpu.VMEM((BLOCK, RANK), f32),
            pltpu.VMEM((16, 8, RANK), f32),
            pltpu.SemaphoreType.DMA((200,)),
            pltpu.SemaphoreType.DMA((200,)),
        ],
        compiler_params=pltpu.CompilerParams(
            collective_id=0, has_side_effects=True, vmem_limit_bytes=63 << 20
        ),
        cost_estimate=pl.CostEstimate(flops=60_000_000_000, bytes_accessed=30 << 20, transcendentals=0),
        name="factors",
    )(momentum, gradient, basis)


def output_kernel(momentum_ref, gradient_ref, rh_ref, rl_ref, oh_ref, sh_ref, sl_ref, momentum_out, update_out):
    rh, rl = rh_ref[...], rl_ref[...]
    dims = (((1,), (1,)), ((), ()))
    low = lax.dot_general(oh_ref[...], rh, dims, preferred_element_type=jnp.float32)
    momentum_out[...] = (momentum_ref[...] + gradient_ref[...].astype(jnp.float32)) - low
    update_out[...] = dot3(sh_ref[...], sl_ref[...], rh, rl, 1, 1).astype(jnp.bfloat16)


def outputs(momentum, gradient, rh, rl, oh, sh, sl):
    rows, columns = momentum.shape
    wide = 256
    tile = pl.BlockSpec((rows, wide), lambda i: (0, i))
    right = pl.BlockSpec((wide, RANK), lambda i: (i, 0))
    whole = pl.BlockSpec((rows, RANK), lambda i: (0, 0))
    return pl.pallas_call(
        output_kernel,
        grid=(columns // wide,),
        out_shape=[
            jax.ShapeDtypeStruct((rows, columns), jnp.float32),
            jax.ShapeDtypeStruct((rows, columns), jnp.bfloat16),
        ],
        in_specs=[tile, tile, right, right, whole, whole, whole],
        out_specs=[tile, tile],
        compiler_params=pltpu.CompilerParams(vmem_limit_bytes=63 << 20),
        name="outputs",
    )(momentum, gradient, rh, rl, oh, sh, sl)


def local(gradient, momentum, basis):
    rh, rl, oh, sh, sl, new_basis = factors(momentum, gradient, basis)
    new_momentum, update = outputs(momentum, gradient, rh, rl, oh, sh, sl)
    return (new_momentum, new_basis, update)


def solution(mesh):
    placed = (P("fsdp", "tp"), P("fsdp", "tp"), P(("tp", "fsdp"), None))
    return jax.shard_map(
        local,
        mesh=mesh,
        in_specs=placed,
        out_specs=(P("fsdp", "tp"), P(("tp", "fsdp"), None), P("fsdp", "tp")),
        check_vma=False,
    )
```
